32 devices in a mesh: row: 4 (over y, x), col: 8 (over z, core).
Axes of the slice: x: 2, y: 2, z: 4, core: 2. Of those that a mesh axis runs over, the one named last changes fastest.
Arguments:
- queries: bfloat16 [2, 64, 128, 2240], P(None, 'row', 'col'), may hold values from -6 to 6
- key_rows_per_head: bfloat16 [2, 64, 128, 2240], P(None, 'row', 'col'), may hold values from -1000 to 1000
- value_rows_per_head: bfloat16 [2, 64, 128, 2240], P(None, 'row', 'col'), may hold values from -13 to 13
- latent_projection_weight: bfloat16 [2240, 32], replicated, may hold values from -0.125 to 0.125
- entry_conv_weight: bfloat16 [3, 3, 32, 512], replicated, may hold values from -0.375 to 0.375
- residual_norm_gain: float32 [512], replicated, may hold values from 0.1 to 1.9
- residual_conv_weight: bfloat16 [3, 3, 512, 512], replicated, may hold values from -0.09375 to 0.09375
- upscale_conv_weight: bfloat16 [3, 3, 512, 512], replicated, may hold values from -0.09375 to 0.09375
Outputs:
- decoded_image: bfloat16 [2, 128, 256, 512], P(None, 'row', 'col')
The draws below stay inside these ranges and needn't reach their ends.
All inputs are finite; a program needn't handle non-finite values.
Results may differ from the reference program's by a relative error of at most 0.017.
Values may be sent and summed in bfloat16 or wider, within the bound.
A program may use at most 128 MiB of HBM per device.

```python
import jax
import jax.numpy as jnp
from jax import lax

HEADS = 70
HEAD = 32
MODEL_WIDTH = 2240
LATENT_CHANNELS = 32
HALF_CHANNELS = 512
C_UP = 512
TILE = 16
IMAGES = 2
TOKEN_ROWS = 64
TOKEN_COLUMNS = 128


def common_draws(key):
    normal_part = jnp.clip(jax.random.normal(key, (IMAGES, TOKEN_ROWS, TOKEN_COLUMNS, MODEL_WIDTH), jnp.float32), -4.0, 4.0)
    return normal_part


def spatial_ramp():
    row_pos = jnp.arange(TOKEN_ROWS, dtype=jnp.float32) / (TOKEN_ROWS - 1)
    col_pos = jnp.arange(TOKEN_COLUMNS, dtype=jnp.float32) / (TOKEN_COLUMNS - 1)
    return (1.0 + 2.0 * row_pos)[:, None] * (1.0 + 2.0 * col_pos)[None, :] / 3.0


def token_scales(key, low, high):
    logs = jax.random.uniform(key, (IMAGES, TOKEN_ROWS, TOKEN_COLUMNS, 1), jnp.float32, jnp.log(low), jnp.log(high))
    return jnp.exp(logs)


def tile_weights(key):
    tile_rows = TOKEN_ROWS // TILE
    tile_cols = TOKEN_COLUMNS // TILE
    tile_count = tile_rows * tile_cols
    heavy_count = max(1, tile_count // 32)
    order = jax.random.permutation(key, tile_count)
    heavy = (order < heavy_count).reshape(tile_rows, tile_cols)
    factor = jnp.where(heavy, 16.0, 1.0).astype(jnp.float32)
    factor = jnp.repeat(jnp.repeat(factor, TILE, axis=0), TILE, axis=1)
    return factor[None, :, :, None]


def draw_key_rows_per_head(key, part):
    normal_part = common_draws(key)
    key = jax.random.fold_in(key, 11)
    heavy = tile_weights(jax.random.fold_in(key, 5))
    base = normal_part
    scales = token_scales(key, 0.5, 5.0)
    return (base * scales * heavy * spatial_ramp()[None, :, :, None]).astype(jnp.bfloat16)


def draw_value_rows_per_head(key, part):
    normal_part = common_draws(key)
    key = jax.random.fold_in(key, 23)
    base = normal_part
    keys_all = jax.random.split(key, 6)
    grouped = base.reshape(IMAGES, TOKEN_ROWS, TOKEN_COLUMNS, HEADS, HEAD)
    first_gain = jax.random.uniform(keys_all[0], (HEADS, HEAD), jnp.float32, 0.3, 1.0)
    second_gain = jax.random.uniform(keys_all[1], (HEADS, HEAD), jnp.float32, -0.6, 0.6)
    third_gain = jax.random.uniform(keys_all[2], (HEADS, HEAD), jnp.float32, -0.6, 0.6)
    mixed = first_gain * grouped + second_gain * jnp.roll(grouped, -1, axis=-1) + third_gain * jnp.roll(grouped, -5, axis=-1)
    row_slope = jax.random.uniform(keys_all[3], (MODEL_WIDTH,), jnp.float32, -1.0, 1.0)
    col_slope = jax.random.uniform(keys_all[4], (MODEL_WIDTH,), jnp.float32, -1.0, 1.0)
    row_pos = 2.0 * jnp.arange(TOKEN_ROWS, dtype=jnp.float32) / (TOKEN_ROWS - 1) - 1.0
    col_pos = 2.0 * jnp.arange(TOKEN_COLUMNS, dtype=jnp.float32) / (TOKEN_COLUMNS - 1) - 1.0
    trend = row_slope * row_pos[:, None, None] + col_slope * col_pos[None, :, None]
    noise = 0.5 * jnp.clip(jax.random.normal(keys_all[5], (IMAGES, TOKEN_ROWS, TOKEN_COLUMNS, MODEL_WIDTH), jnp.float32), -4.0, 4.0)
    return (mixed.reshape(IMAGES, TOKEN_ROWS, TOKEN_COLUMNS, MODEL_WIDTH) + trend[None] + noise).astype(jnp.bfloat16)


def shard_levels(key, extent, cuts, low, high):
    def one(axis_at, parts):
        draws = jax.random.uniform(jax.random.fold_in(jax.random.fold_in(key, 6), axis_at), (parts,), jnp.float32, low / len(cuts), high / len(cuts))
        return jnp.repeat(jnp.exp(draws), extent[axis_at] // parts).reshape((-1,) + (1,) * (len(extent) - axis_at - 1))

    gain = one(*cuts[0])
    for cut in cuts[1:]:
        gain = gain * one(*cut)
    return gain


def normal_values(key, dims, deviation, most, shards=(), kind=jnp.bfloat16):
    level = shard_levels(key, dims, shards, -0.22, 0.18) if shards else 1.0
    result = jax.random.normal(key, dims, jnp.float32) * deviation * level
    return jnp.minimum(jnp.maximum(result, -most), most).astype(kind)


def setup_inputs(seed: int = 0) -> dict:
    key_list = jax.random.split(jax.random.key(seed), 9)
    return {
        "queries": normal_values(key_list[0], (IMAGES, TOKEN_ROWS, TOKEN_COLUMNS, MODEL_WIDTH), 1.0, 6.0, ((1, 4), (2, 8))),
        "key_rows_per_head": draw_key_rows_per_head(jax.random.fold_in(key_list[8], 71), 0),
        "value_rows_per_head": draw_value_rows_per_head(jax.random.fold_in(key_list[8], 71), 0),
        "latent_projection_weight": normal_values(key_list[3], (MODEL_WIDTH, LATENT_CHANNELS), MODEL_WIDTH ** -0.5, 0.125),
        "entry_conv_weight": normal_values(key_list[4], (3, 3, LATENT_CHANNELS, HALF_CHANNELS), (9 * LATENT_CHANNELS) ** -0.5, 0.375),
        "residual_norm_gain": jnp.clip(1.0 + 0.18 * jax.random.normal(key_list[5], (HALF_CHANNELS,), jnp.float32), 0.1, 1.9),
        "residual_conv_weight": normal_values(key_list[6], (3, 3, HALF_CHANNELS, HALF_CHANNELS), (9 * HALF_CHANNELS) ** -0.5, 0.09375),
        "upscale_conv_weight": normal_values(key_list[7], (3, 3, HALF_CHANNELS, C_UP), (9 * HALF_CHANNELS) ** -0.5, 0.09375),
    }


NORM_EPS = 1e-06

def convolve_padded(inputs, weights):
    return lax.conv_general_dilated(inputs.astype(jnp.float32), weights.astype(jnp.float32), (1, 1), ((1, 1), (1, 1)), dimension_numbers=('NHWC', 'HWIO', 'NHWC'))

def activate(decoder_output, residual_norm_gain):
    values_f = decoder_output.astype(jnp.float32)
    scaled = values_f * lax.rsqrt(lax.optimization_barrier(jnp.mean(values_f * values_f, axis=-1, keepdims=True)) + NORM_EPS) * residual_norm_gain.astype(jnp.float32)
    return jax.nn.silu(scaled).astype(jnp.bfloat16)

def attend_image(query_img, key_img, value_img, latent_projection_weight):
    token_count = TOKEN_ROWS * TOKEN_COLUMNS
    relu_keys = jnp.maximum(key_img.astype(jnp.float32), 0.0).reshape(token_count, HEADS, HEAD)
    head_values = value_img.astype(jnp.float32).reshape(token_count, HEADS, HEAD)
    key_value = jnp.einsum('nhi,nhj->hij', relu_keys, head_values) / token_count
    key_mean = lax.optimization_barrier(jnp.sum(relu_keys, axis=0)) / token_count
    key_value = lax.optimization_barrier(key_value.astype(jnp.bfloat16)).astype(jnp.float32)
    key_mean = lax.optimization_barrier(key_mean.astype(jnp.bfloat16)).astype(jnp.float32)
    relu_query = jnp.maximum(query_img.astype(jnp.float32), 0.0).reshape(token_count, HEADS, HEAD)
    numerator = jnp.einsum('nhi,hij->nhj', relu_query, key_value)
    denominator = jnp.einsum('nhi,hi->nh', relu_query, key_mean)
    attended = (numerator / jnp.maximum(denominator, 1.0)[:, :, None]).reshape(token_count, MODEL_WIDTH)
    normed = (attended * lax.rsqrt(lax.optimization_barrier(jnp.mean(attended * attended, axis=1, keepdims=True)) + NORM_EPS)).astype(jnp.bfloat16)
    latent_state = jnp.dot(normed, latent_projection_weight, preferred_element_type=jnp.float32).astype(jnp.bfloat16)
    return latent_state.reshape(TOKEN_ROWS, TOKEN_COLUMNS, LATENT_CHANNELS)

def reference(queries, key_rows_per_head, value_rows_per_head, latent_projection_weight, entry_conv_weight, residual_norm_gain, residual_conv_weight, upscale_conv_weight):
    latent_state = lax.map(lambda operands: attend_image(operands[0], operands[1], operands[2], latent_projection_weight), (queries, key_rows_per_head, value_rows_per_head))
    decoder_output = convolve_padded(latent_state, entry_conv_weight).astype(jnp.bfloat16)
    hidden_state = activate(decoder_output, residual_norm_gain)
    residual_output = (decoder_output.astype(jnp.float32) + convolve_padded(hidden_state, residual_conv_weight)).astype(jnp.bfloat16)
    upsampled = jnp.repeat(jnp.repeat(residual_output, 2, axis=1), 2, axis=2)
    return convolve_padded(upsampled, upscale_conv_weight).astype(jnp.bfloat16)
```

```python
import functools

import jax
import jax.numpy as jnp
from jax import lax
from jax.experimental import pallas as pl
from jax.experimental.pallas import tpu as pltpu
from jax.sharding import PartitionSpec as P

HEAD = 32
NORM_EPS = 1e-06
LANES = 128
HALO = 3
SLOT = 24
MESH = pl.DeviceIdType.MESH
F32 = jnp.float32
BF16 = jnp.bfloat16
AROUND = ((-1, -1), (-1, 0), (-1, 1), (0, -1), (0, 1), (1, -1), (1, 0), (1, 1))


def contract(a, b, dim_a, dim_b):
    return lax.dot_general(a, b, (((dim_a,), (dim_b,)), ((), ())), preferred_element_type=F32)


def same_head(shape):
    return lax.broadcasted_iota(jnp.int32, shape, 0) // HEAD == lax.broadcasted_iota(
        jnp.int32, shape, 1
    ) // HEAD


def attention_kernel(
    rows, cols, tile, width, per_chip,
    k_hbm, v_hbm, q_hbm, proj_hbm, ext_ref,
    k_buf, v_buf, q_buf, proj, part, other, chip_sum, arrived, total, lat, strips, halo,
    in_sem, swap_sem, rs_send, rs_recv, ag_send, ag_recv, halo_send, halo_recv,
):
    row, col = lax.axis_index("row"), lax.axis_index("col")
    core = lax.rem(col, 2)
    zs = cols // 2
    chips = rows * zs
    chip = row * zs + col // 2
    me = row * cols + col
    tokens = tile * tile
    blocks = -(-width // LANES)
    token_count = float(tokens * rows * cols)

    def place(c):
        return (c // zs, lax.rem(c, zs) * 2 + core)

    partner = (row, col + 1 - 2 * core)

    loads = {}
    for step in range(2):
        image = (1 - core) if step == 0 else core
        loads["k", step] = pltpu.make_async_copy(k_hbm.at[image], k_buf.at[image], in_sem.at[step])
        loads["v", step] = pltpu.make_async_copy(v_hbm.at[image], v_buf.at[image], in_sem.at[2 + step])
    load_proj = pltpu.make_async_copy(proj_hbm, proj, in_sem.at[4])
    load_q = pltpu.make_async_copy(q_hbm, q_buf, in_sem.at[5])
    for copy in loads.values():
        copy.start()
    load_proj.start()
    load_q.start()

    barrier = pltpu.get_barrier_semaphore()

    def greet(d, carry):
        t = lax.rem(me + d, rows * cols)
        pl.semaphore_signal(
            barrier, inc=1, device_id=(t // cols, lax.rem(t, cols)), device_id_type=MESH
        )
        return carry

    lax.fori_loop(1, rows * cols, greet, 0)

    units = chips * per_chip
    part[:, 2 * blocks :] = jnp.zeros((2, units - 2 * blocks, 16, LANES), F32)
    mask = same_head((LANES, LANES))

    def sums(image):
        for b in range(blocks):
            lo = b * LANES
            w = min(LANES, width - lo)
            keys = jnp.maximum(k_buf[image, :, lo : lo + w], 0)
            values = v_buf[image, :, lo : lo + w]
            full = jnp.where(mask[:w, :w], contract(values, keys, 0, 0), 0.0)
            packed = full[0:HEAD]
            for h in range(1, w // HEAD):
                packed = packed + full[h * HEAD : (h + 1) * HEAD]
            mean = jnp.sum(keys.astype(F32), axis=0, keepdims=True)
            part[image, 2 * b, :, 0:w] = packed[0:16]
            part[image, 2 * b + 1, :, 0:w] = packed[16:32]
            part[image, 2 * blocks + b // 16, b % 16 : b % 16 + 1, 0:w] = mean

    loads["k", 0].wait()
    loads["v", 0].wait()
    sums(1 - core)
    pl.semaphore_wait(barrier, rows * cols - 1)
    swap = pltpu.make_async_remote_copy(
        src_ref=part.at[1 - core], dst_ref=other, send_sem=swap_sem.at[0],
        recv_sem=swap_sem.at[1], device_id=partner, device_id_type=MESH,
    )
    swap.start()
    loads["k", 1].wait()
    loads["v", 1].wait()
    sums(core)
    swap.wait()
    chip_sum[...] = (part[core] + other[...]).reshape(chips, per_chip, 16, LANES).astype(BF16)

    def scatter(k):
        t = lax.rem(chip + k, chips)
        return pltpu.make_async_remote_copy(
            src_ref=chip_sum.at[t], dst_ref=arrived.at[chip], send_sem=rs_send.at[k],
            recv_sem=rs_recv.at[chip], device_id=place(t), device_id_type=MESH,
        )

    def scatter_from(k):
        t = lax.rem(chip + k, chips)
        return t, pltpu.make_async_remote_copy(
            src_ref=chip_sum.at[t], dst_ref=arrived.at[t], send_sem=rs_send.at[k],
            recv_sem=rs_recv.at[t], device_id=place(t), device_id_type=MESH,
        )

    def gather(k):
        t = lax.rem(chip + k, chips)
        return pltpu.make_async_remote_copy(
            src_ref=total.at[core, chip], dst_ref=total.at[core, chip], send_sem=ag_send.at[k],
            recv_sem=ag_recv.at[chip], device_id=place(t), device_id_type=MESH,
        )

    def gather_from(k):
        t = lax.rem(chip + k, chips)
        return pltpu.make_async_remote_copy(
            src_ref=total.at[core, t], dst_ref=total.at[core, t], send_sem=ag_send.at[k],
            recv_sem=ag_recv.at[t], device_id=place(t), device_id_type=MESH,
        )

    def each(body):
        def step(k, carry):
            body(k)
            return carry

        lax.fori_loop(1, chips, step, 0)

    each(lambda k: scatter(k).start())

    def add(k, acc):
        t, copy = scatter_from(k)
        copy.wait_recv()
        return acc + arrived[t].astype(F32)

    acc = lax.fori_loop(1, chips, add, chip_sum[chip].astype(F32))
    total[core, chip] = (acc / token_count).astype(BF16)
    each(lambda k: gather(k).start())
    each(lambda k: gather_from(k).wait_recv())
    swap_back = pltpu.make_async_remote_copy(
        src_ref=total.at[core], dst_ref=total.at[core], send_sem=swap_sem.at[2],
        recv_sem=swap_sem.at[3], device_id=partner, device_id_type=MESH,
    )
    swap_back.start()
    load_q.wait()
    load_proj.wait()

    def unit(image, u, lo=0, hi=16):
        return total[image, u // per_chip, u % per_chip]

    def attend(image):
        squares = jnp.zeros((tokens, 1), F32)
        out = jnp.zeros((tokens, HEAD), F32)
        means = [
            unit(image, 2 * blocks + i).astype(F32) for i in range(-(-blocks // 16))
        ]
        for b in range(blocks):
            lo = b * LANES
            w = min(LANES, width - lo)
            packed = jnp.concatenate(
                [unit(image, 2 * b).astype(F32), unit(image, 2 * b + 1).astype(F32)], axis=0
            )
            spread = jnp.where(mask, jnp.concatenate([packed] * (LANES // HEAD), axis=0), 0.0)
            mean = means[b // 16][b % 16 : b % 16 + 1]
            spread_mean = jnp.where(mask, jnp.broadcast_to(mean, (LANES, LANES)), 0.0)
            both = jnp.concatenate([spread, spread_mean], axis=0).astype(BF16)
            query = jnp.maximum(q_buf[image, :, lo : lo + w], 0)
            result = contract(query, both[:, :w], 1, 1)
            attended = result[:, :w] / jnp.maximum(result[:, LANES : LANES + w], 1.0)
            squares = squares + jnp.sum(attended * attended, axis=1, keepdims=True)
            out = out + contract(attended.astype(BF16), proj[:, lo : lo + w], 1, 1)
        out = out * lax.rsqrt(squares / width + NORM_EPS)
        out = out.astype(BF16).astype(F32)
        lat[pl.ds(image * tokens, tokens)] = jnp.concatenate(
            [out, jnp.zeros((tokens, LANES - HEAD), F32)], axis=1
        )

    attend(core)
    swap_back.wait()
    attend(1 - core)

    ext_ref[...] = jnp.zeros(ext_ref.shape, F32)
    line = 2 * SLOT

    def pack(pieces):
        packed = pieces[0]
        for i in range(1, HALO):
            packed = packed + pltpu.roll(pieces[i], i * HEAD, 1)
        return packed.astype(BF16)

    def rows_of(first):
        return pack([
            jnp.concatenate(
                [lat[i * tokens + (first + r) * tile : i * tokens + (first + r + 1) * tile] for i in range(2)],
                axis=0,
            )
            for r in range(HALO)
        ])

    def cols_of(first):
        return pack([lat[pl.ds(first + c, 2 * tile, stride=tile)] for c in range(HALO)])

    strips[0] = rows_of(0)
    strips[1] = rows_of(tile - HALO)
    strips[2] = cols_of(0)
    strips[3] = cols_of(tile - HALO)

    def exchange(d):
        dr, dc = AROUND[d]
        source = (0 if dr < 0 else 1) if dr else (2 if dc < 0 else 3)
        there = (
            (row + dr >= 0) & (row + dr < rows) & (col + dc >= 0) & (col + dc < cols)
        )
        return there, pltpu.make_async_remote_copy(
            src_ref=strips.at[source], dst_ref=halo.at[7 - d], send_sem=halo_send.at[d],
            recv_sem=halo_recv.at[7 - d], device_id=(row + dr, col + dc), device_id_type=MESH,
        )

    def exchange_from(d):
        dr, dc = AROUND[d]
        there = (
            (row + dr >= 0) & (row + dr < rows) & (col + dc >= 0) & (col + dc < cols)
        )
        return there, pltpu.make_async_remote_copy(
            src_ref=strips.at[0], dst_ref=halo.at[d], send_sem=halo_send.at[d],
            recv_sem=halo_recv.at[d], device_id=(row + dr, col + dc), device_id_type=MESH,
        )

    for d in range(8):
        there, copy = exchange(d)
        pl.when(there)(copy.start)

    for i in range(2):
        for y in range(tile):
            ext_ref[pl.ds((y + HALO) * line + i * SLOT + HALO, tile)] = lat[
                i * tokens + y * tile : i * tokens + (y + 1) * tile
            ]

    lane = lax.broadcasted_iota(jnp.int32, (2 * tile, LANES), 1)

    def take(d):
        dr, dc = AROUND[d]
        packed = halo[d].astype(F32)
        for n in range(HALO):
            piece = packed if n == 0 else pltpu.roll(packed, LANES - n * HEAD, 1)
            piece = jnp.where(lane < HEAD, piece, 0.0)
            for i in range(2):
                one = piece[i * tile : (i + 1) * tile]
                if dr:
                    y = n if dr < 0 else HALO + tile + n
                    at = y * line + i * SLOT
                    if dc < 0:
                        ext_ref[pl.ds(at, HALO)] = one[tile - HALO :]
                    elif dc == 0:
                        ext_ref[pl.ds(at + HALO, tile)] = one
                    else:
                        ext_ref[pl.ds(at + HALO + tile, HALO)] = one[:HALO]
                else:
                    x = n if dc < 0 else HALO + tile + n
                    ext_ref[pl.ds(HALO * line + i * SLOT + x, tile, stride=line)] = one

    for d in range(8):
        there, copy = exchange_from(d)

        @pl.when(there)
        def _(copy=copy, d=d):
            copy.wait_recv()
            take(d)

    each(lambda k: scatter(k).wait_send())
    each(lambda k: gather(k).wait_send())
    for d in range(8):
        there, copy = exchange(d)
        pl.when(there)(copy.wait_send)


def decoder_kernel(
    rows, cols, tile, ext_ref, entry_ref, gain_ref, res_ref, up_ref, out_ref,
    cat, hid, dec, ref_, shifted, sums, woven,
):
    row, col = lax.axis_index("row"), lax.axis_index("col")
    line = 2 * SLOT
    wide = tile + 2 * HALO
    chan = res_ref.shape[-1]

    def inside(reach, first, count):
        p = first + lax.broadcasted_iota(jnp.int32, (count, 1), 0)
        y, x = p // line - reach, lax.rem(lax.rem(p, line), SLOT) - reach
        gy, gx = row * tile + y, col * tile + x
        return (gy >= 0) & (gy < rows * tile) & (gx >= 0) & (gx < cols * tile)

    ext = ext_ref[...]
    n_ext = wide * line
    packed = ext
    for d in range(1, 3):
        packed = packed + pltpu.roll(pltpu.roll(ext, n_ext - d, 0), d * HEAD, 1)
    cat[...] = packed.astype(BF16)

    n_dec = (wide - 2) * line
    gain = gain_ref[...]
    half = n_dec // 2
    for part in range(2):
        lo = part * half
        acc = jnp.zeros((half, chan), F32)
        for dy in range(3):
            acc = acc + contract(
                cat[lo + dy * line : lo + dy * line + half, : 3 * HEAD], entry_ref[dy], 1, 0
            )
        value = acc.astype(BF16).astype(F32)
        dec[lo : lo + half] = value
        scaled = value * lax.rsqrt(jnp.mean(value * value, axis=1, keepdims=True) + NORM_EPS) * gain
        active = jnp.where(inside(2, lo, half), scaled * jax.nn.sigmoid(scaled), 0.0)
        hid[lo : lo + half, 0:chan] = active.astype(BF16)
    whole = hid[:, 0:chan].astype(F32)
    for d in range(1, 3):
        hid[:, d * chan : (d + 1) * chan] = pltpu.roll(whole, n_dec - d, 0).astype(BF16)

    n_ref = (wide - 4) * line
    tiles = 2
    step = n_ref // tiles
    rows_each = chan // tiles

    def residual(i, carry):
        lo = pl.multiple_of(i * step, 16)
        acc = jnp.zeros((step, chan), F32)
        for dy in range(3):
            acc = acc + contract(hid[pl.ds(pl.multiple_of(lo + dy * line, 16), step), :], res_ref[dy], 1, 0)
        center = pltpu.roll(dec[pl.ds(pl.multiple_of(lo + line, 8), step + 8), :], step + 7, 0)[:step]
        refined = (acc + center).astype(BF16).astype(F32)
        ref_[pl.ds(lo, step), :] = jnp.where(inside(1, lo, step), refined, 0.0)
        at = pl.ds(pl.multiple_of(i * rows_each, 16), rows_each)
        by_row = []
        for c in range(3):
            w = [up_ref[r, c, at, :].astype(F32) for r in range(3)]
            by_row.append((w[0], w[1] + w[2], w[0] + w[1], w[2]))
        for a in range(4):
            w = [by_row[c][a] for c in range(3)]
            for b, value in enumerate((w[0], w[1] + w[2], w[0] + w[1], w[2])):
                sums[a, b, at, :] = value.astype(BF16)
        return carry

    lax.fori_loop(0, tiles, residual, 0)

    for y in range(tile + 2):
        for i in range(2):
            part = ref_[y * line + i * SLOT : y * line + (i + 1) * SLOT]
            for d in range(3):
                moved = part if d == 0 else pltpu.roll(part, SLOT - d, 0)
                shifted[d, (y * 2 + i) * tile : (y * 2 + i + 1) * tile, :] = moved[:tile].astype(BF16)

    count = tile * 2 * tile
    for a in range(2):
        for b in range(2):
            acc = jnp.zeros((count, chan), F32)
            for di in range(2):
                for dj in range(2):
                    lo = (a + di) * 2 * tile
                    acc = acc + contract(
                        shifted[b + dj, lo : lo + count, :], sums[2 * a + di, 2 * b + dj], 1, 0
                    )
            for n in range(chan // LANES):
                woven[n, pl.ds(b, count, stride=2), :] = acc[:, n * LANES : (n + 1) * LANES]
        for n in range(chan // LANES):
            value = woven[n].astype(BF16).reshape(tile, 2, 2 * tile, LANES)
            for i in range(2):
                out_ref[i, :, a, :, n * LANES : (n + 1) * LANES] = value[:, i]


def local(rows, cols, q, k, v, proj, entry, gain, res, up):
    images, tile, _, width = q.shape
    chan = res.shape[-1]
    tokens = tile * tile
    chips = rows * cols // 2
    blocks = -(-width // LANES)
    per_chip = -(-(2 * blocks + -(-blocks // 16)) // chips)
    wide = tile + 2 * HALO
    line = 2 * SLOT
    vmem = pl.BlockSpec(memory_space=pltpu.VMEM)
    hbm = pl.BlockSpec(memory_space=pl.ANY)
    flat = (images, tokens, width)
    unit = (16, LANES)
    dma = pltpu.SemaphoreType.DMA
    ext = pl.pallas_call(
        functools.partial(attention_kernel, rows, cols, tile, width, per_chip),
        out_shape=jax.ShapeDtypeStruct((wide * line, LANES), F32),
        in_specs=[hbm] * 4,
        out_specs=vmem,
        scratch_shapes=[
            pltpu.VMEM(flat, BF16), pltpu.VMEM(flat, BF16), pltpu.VMEM(flat, BF16),
            pltpu.VMEM((proj.shape[1], width), BF16),
            pltpu.VMEM((images, chips * per_chip) + unit, F32),
            pltpu.VMEM((chips * per_chip,) + unit, F32),
            pltpu.VMEM((chips, per_chip) + unit, BF16),
            pltpu.VMEM((chips, per_chip) + unit, BF16),
            pltpu.VMEM((images, chips, per_chip) + unit, BF16),
            pltpu.VMEM((images * tokens, LANES), F32),
            pltpu.VMEM((4, 2 * tile, LANES), BF16),
            pltpu.VMEM((8, 2 * tile, LANES), BF16),
            dma((6,)), dma((4,)), dma((chips,)), dma((chips,)), dma((chips,)), dma((chips,)),
            dma((8,)), dma((8,)),
        ],
        compiler_params=pltpu.CompilerParams(
            collective_id=0, has_side_effects=True, vmem_limit_bytes=32 * 1024 * 1024
        ),
        name="attention",
    )(k.reshape(flat), v.reshape(flat), q.reshape(flat), proj.T)
    count = tile * 2 * tile
    out = pl.pallas_call(
        functools.partial(decoder_kernel, rows, cols, tile),
        out_shape=jax.ShapeDtypeStruct((images, tile, 2, 2 * tile, chan), BF16),
        in_specs=[vmem] * 5,
        out_specs=vmem,
        scratch_shapes=[
            pltpu.VMEM((wide * line, LANES), BF16),
            pltpu.VMEM(((wide - 2) * line, 3 * chan), BF16),
            pltpu.VMEM(((wide - 2) * line, chan), F32),
            pltpu.VMEM(((wide - 4) * line, chan), F32),
            pltpu.VMEM((3, (tile + 2) * 2 * tile, chan), BF16),
            pltpu.VMEM((4, 4, chan, chan), BF16),
            pltpu.VMEM((chan // LANES, 2 * count, LANES), F32),
        ],
        compiler_params=pltpu.CompilerParams(vmem_limit_bytes=44 * 1024 * 1024),
        name="decoder",
    )(ext, entry.reshape(3, -1, chan), gain.reshape(1, chan), res.reshape(3, -1, chan), up)
    return out.reshape(images, 2 * tile, 2 * tile, chan)


def solution(mesh):
    spread = P(None, "row", "col", None)
    rows, cols = mesh.shape["row"], mesh.shape["col"]
    return jax.shard_map(
        functools.partial(local, rows, cols),
        mesh=mesh,
        in_specs=(spread,) * 3 + (P(),) * 5,
        out_specs=spread,
        check_vma=False,
    )
```

```python
import functools

import jax
import jax.numpy as jnp
from jax import lax
from jax.experimental import pallas as pl
from jax.experimental.pallas import tpu as pltpu
from jax.sharding import PartitionSpec as P

HEAD = 32
NORM_EPS = 1e-06
LANES = 128
HALO = 3
SLOT = 24
MESH = pl.DeviceIdType.MESH
F32 = jnp.float32
BF16 = jnp.bfloat16
AROUND = ((-1, -1), (-1, 0), (-1, 1), (0, -1), (0, 1), (1, -1), (1, 0), (1, 1))


def contract(a, b, dim_a, dim_b):
    return lax.dot_general(a, b, (((dim_a,), (dim_b,)), ((), ())), preferred_element_type=F32)


def same_head(shape):
    return lax.broadcasted_iota(jnp.int32, shape, 0) // HEAD == lax.broadcasted_iota(
        jnp.int32, shape, 1
    ) // HEAD


def attention_kernel(
    rows, cols, tile, width, per_chip,
    k_hbm, v_hbm, q_hbm, proj_hbm, ext_ref,
    k_buf, v_buf, q_buf, proj, part, other, chip_sum, arrived, total, lat, strips, halo,
    in_sem, swap_sem, rs_send, rs_recv, ag_send, ag_recv, halo_send, halo_recv, fw_send, fw_recv,
):
    row, col = lax.axis_index("row"), lax.axis_index("col")
    core = lax.rem(col, 2)
    zs = cols // 2
    chips = rows * zs
    chip = row * zs + col // 2
    me = row * cols + col
    tokens = tile * tile
    blocks = -(-width // LANES)
    token_count = float(tokens * rows * cols)

    def place(c):
        return (c // zs, lax.rem(c, zs) * 2 + core)

    partner = (row, col + 1 - 2 * core)

    loads = {}
    for step in range(2):
        image = (1 - core) if step == 0 else core
        loads["k", step] = pltpu.make_async_copy(k_hbm.at[image], k_buf.at[image], in_sem.at[step])
        loads["v", step] = pltpu.make_async_copy(v_hbm.at[image], v_buf.at[image], in_sem.at[2 + step])
    load_proj = pltpu.make_async_copy(proj_hbm, proj, in_sem.at[4])
    load_q = pltpu.make_async_copy(q_hbm, q_buf, in_sem.at[5])
    for copy in loads.values():
        copy.start()
    load_proj.start()
    load_q.start()

    barrier = pltpu.get_barrier_semaphore()

    def greet(d, carry):
        t = lax.rem(me + d, rows * cols)
        pl.semaphore_signal(
            barrier, inc=1, device_id=(t // cols, lax.rem(t, cols)), device_id_type=MESH
        )
        return carry

    lax.fori_loop(1, rows * cols, greet, 0)

    lead = -(-blocks // 16)
    units = lead + 2 * blocks
    owners = -(-units // per_chip)
    part[:, :lead] = jnp.zeros((2, lead, 16, LANES), F32)
    part[:, units:] = jnp.zeros((2, chips * per_chip - units, 16, LANES), F32)
    mask = same_head((LANES, LANES))

    def sums(image):
        for b in range(blocks):
            lo = b * LANES
            w = min(LANES, width - lo)
            keys = jnp.maximum(k_buf[image, :, lo : lo + w], 0)
            values = v_buf[image, :, lo : lo + w]
            full = jnp.where(mask[:w, :w], contract(values, keys, 0, 0), 0.0)
            packed = full[0:HEAD]
            for h in range(1, w // HEAD):
                packed = packed + full[h * HEAD : (h + 1) * HEAD]
            mean = jnp.sum(keys.astype(F32), axis=0, keepdims=True)
            if w < LANES:
                packed = jnp.concatenate([packed, jnp.zeros((HEAD, LANES - w), F32)], axis=1)
            part[image, lead + 2 * b] = packed[0:16]
            part[image, lead + 2 * b + 1] = packed[16:32]
            part[image, b // 16, b % 16 : b % 16 + 1, 0:w] = mean

    loads["k", 0].wait()
    loads["v", 0].wait()
    sums(1 - core)
    pl.semaphore_wait(barrier, rows * cols - 1)
    swap = pltpu.make_async_remote_copy(
        src_ref=part.at[1 - core], dst_ref=other, send_sem=swap_sem.at[0],
        recv_sem=swap_sem.at[1], device_id=partner, device_id_type=MESH,
    )
    swap.start()
    loads["k", 1].wait()
    loads["v", 1].wait()
    sums(core)
    swap.wait()
    chip_sum[...] = (part[core] + other[...]).reshape(chips, per_chip, 16, LANES).astype(BF16)

    def scatter(k):
        t = lax.rem(chip + k, chips)
        return pltpu.make_async_remote_copy(
            src_ref=chip_sum.at[t], dst_ref=arrived.at[chip], send_sem=rs_send.at[k],
            recv_sem=rs_recv.at[chip], device_id=place(t), device_id_type=MESH,
        )

    def scatter_from(k):
        t = lax.rem(chip + k, chips)
        return t, pltpu.make_async_remote_copy(
            src_ref=chip_sum.at[t], dst_ref=arrived.at[t], send_sem=rs_send.at[k],
            recv_sem=rs_recv.at[t], device_id=place(t), device_id_type=MESH,
        )

    def gather(k):
        t = lax.rem(chip + k, chips)
        return pltpu.make_async_remote_copy(
            src_ref=total.at[core, chip], dst_ref=total.at[core, chip], send_sem=ag_send.at[k],
            recv_sem=ag_recv.at[chip], device_id=place(t), device_id_type=MESH,
        )

    def each(body):
        def step(k, carry):
            body(k)
            return carry

        lax.fori_loop(1, chips, step, 0)

    def owner(k):
        return lax.rem(chip + k, chips) < owners

    each(lambda k: pl.when(owner(k))(scatter(k).start))

    def add(k, acc):
        t, copy = scatter_from(k)
        copy.wait_recv()
        return acc + arrived[t].astype(F32)

    def forward(t):
        return pltpu.make_async_remote_copy(
            src_ref=total.at[core, t], dst_ref=total.at[core, t], send_sem=fw_send.at[t],
            recv_sem=fw_recv.at[t], device_id=partner, device_id_type=MESH,
        )

    def forwarded(t):
        return pltpu.make_async_remote_copy(
            src_ref=total.at[1 - core, t], dst_ref=total.at[1 - core, t], send_sem=fw_send.at[t],
            recv_sem=fw_recv.at[t], device_id=partner, device_id_type=MESH,
        )

    @pl.when(chip < owners)
    def _():
        acc = lax.fori_loop(1, chips, add, chip_sum[chip].astype(F32))
        total[core, chip] = (acc / token_count).astype(BF16)
        each(lambda k: gather(k).start())

    def receive(t):
        @pl.when(chip != t)
        def _():
            pltpu.make_async_remote_copy(
                src_ref=total.at[core, t], dst_ref=total.at[core, t], send_sem=ag_send.at[0],
                recv_sem=ag_recv.at[t], device_id=place(t), device_id_type=MESH,
            ).wait_recv()

        forward(t).start()

    def receive_forwarded(t):
        forwarded(t).wait_recv()

    load_q.wait()
    load_proj.wait()

    def attend(image, get):
        squares = jnp.zeros((tokens, LANES), F32)
        out = jnp.zeros((tokens, HEAD), F32)
        held = 0

        def unit(u):
            return total[image, u // per_chip, u % per_chip].astype(F32)

        for b in range(blocks):
            while held * per_chip < lead + 2 * b + 2:
                get(held)
                held += 1
            lo = b * LANES
            w = min(LANES, width - lo)
            packed = jnp.concatenate([unit(lead + 2 * b), unit(lead + 2 * b + 1)], axis=0)
            spread = jnp.where(mask, jnp.concatenate([packed] * (LANES // HEAD), axis=0), 0.0)
            mean = unit(b // 16)[b % 16 : b % 16 + 1]
            spread_mean = jnp.where(mask, jnp.broadcast_to(mean, (LANES, LANES)), 0.0)
            both = jnp.concatenate([spread, spread_mean], axis=0).astype(BF16)
            query = jnp.maximum(q_buf[image, :, lo : lo + w], 0)
            result = contract(query, both[:, :w], 1, 1)
            attended = result[:, :LANES] / jnp.maximum(result[:, LANES:], 1.0)
            squares = squares + attended * attended
            out = out + contract(attended[:, :w].astype(BF16), proj[:, lo : lo + w], 1, 1)
        out = out * lax.rsqrt(jnp.sum(squares, axis=1, keepdims=True) / width + NORM_EPS)
        out = out.astype(BF16).astype(F32)
        lat[pl.ds(image * tokens, tokens)] = jnp.concatenate(
            [out, jnp.zeros((tokens, LANES - HEAD), F32)], axis=1
        )

    attend(core, receive)
    attend(1 - core, receive_forwarded)

    ext_ref[...] = jnp.zeros(ext_ref.shape, F32)
    line = 2 * SLOT

    def pack(pieces):
        packed = pieces[0]
        for i in range(1, HALO):
            packed = packed + pltpu.roll(pieces[i], i * HEAD, 1)
        return packed.astype(BF16)

    def rows_of(first):
        return pack([
            jnp.concatenate(
                [lat[i * tokens + (first + r) * tile : i * tokens + (first + r + 1) * tile] for i in range(2)],
                axis=0,
            )
            for r in range(HALO)
        ])

    def cols_of(first):
        return pack([lat[pl.ds(first + c, 2 * tile, stride=tile)] for c in range(HALO)])

    strips[0] = rows_of(0)
    strips[1] = rows_of(tile - HALO)
    strips[2] = cols_of(0)
    strips[3] = cols_of(tile - HALO)

    def exchange(d):
        dr, dc = AROUND[d]
        source = (0 if dr < 0 else 1) if dr else (2 if dc < 0 else 3)
        there = (
            (row + dr >= 0) & (row + dr < rows) & (col + dc >= 0) & (col + dc < cols)
        )
        return there, pltpu.make_async_remote_copy(
            src_ref=strips.at[source], dst_ref=halo.at[7 - d], send_sem=halo_send.at[d],
            recv_sem=halo_recv.at[7 - d], device_id=(row + dr, col + dc), device_id_type=MESH,
        )

    def exchange_from(d):
        dr, dc = AROUND[d]
        there = (
            (row + dr >= 0) & (row + dr < rows) & (col + dc >= 0) & (col + dc < cols)
        )
        return there, pltpu.make_async_remote_copy(
            src_ref=strips.at[0], dst_ref=halo.at[d], send_sem=halo_send.at[d],
            recv_sem=halo_recv.at[d], device_id=(row + dr, col + dc), device_id_type=MESH,
        )

    for d in range(8):
        there, copy = exchange(d)
        pl.when(there)(copy.start)

    for i in range(2):
        for y in range(tile):
            ext_ref[pl.ds((y + HALO) * line + i * SLOT + HALO, tile)] = lat[
                i * tokens + y * tile : i * tokens + (y + 1) * tile
            ]

    lane = lax.broadcasted_iota(jnp.int32, (2 * tile, LANES), 1)

    def take(d):
        dr, dc = AROUND[d]
        packed = halo[d].astype(F32)
        for n in range(HALO):
            piece = packed if n == 0 else pltpu.roll(packed, LANES - n * HEAD, 1)
            piece = jnp.where(lane < HEAD, piece, 0.0)
            for i in range(2):
                one = piece[i * tile : (i + 1) * tile]
                if dr:
                    y = n if dr < 0 else HALO + tile + n
                    at = y * line + i * SLOT
                    if dc < 0:
                        ext_ref[pl.ds(at, HALO)] = one[tile - HALO :]
                    elif dc == 0:
                        ext_ref[pl.ds(at + HALO, tile)] = one
                    else:
                        ext_ref[pl.ds(at + HALO + tile, HALO)] = one[:HALO]
                else:
                    x = n if dc < 0 else HALO + tile + n
                    ext_ref[pl.ds(HALO * line + i * SLOT + x, tile, stride=line)] = one

    for d in range(8):
        there, copy = exchange_from(d)

        @pl.when(there)
        def _(copy=copy, d=d):
            copy.wait_recv()
            take(d)

    each(lambda k: pl.when(owner(k))(scatter(k).wait_send))
    pl.when(chip < owners)(lambda: each(lambda k: gather(k).wait_send()))
    for t in range(owners):
        forward(t).wait_send()
    for d in range(8):
        there, copy = exchange(d)
        pl.when(there)(copy.wait_send)


def decoder_kernel(
    rows, cols, tile, ext_ref, entry_ref, gain_ref, res_ref, up_hbm, out_ref,
    up_ref, cat, hid, dec, ref_, shifted, sums, woven, up_sem,
):
    load_up = pltpu.make_async_copy(up_hbm, up_ref, up_sem)
    load_up.start()
    row, col = lax.axis_index("row"), lax.axis_index("col")
    line = 2 * SLOT
    wide = tile + 2 * HALO
    chan = res_ref.shape[-1]

    def inside(reach, first, count):
        p = first + lax.broadcasted_iota(jnp.int32, (count, 1), 0)
        y, x = p // line - reach, lax.rem(lax.rem(p, line), SLOT) - reach
        gy, gx = row * tile + y, col * tile + x
        return (gy >= 0) & (gy < rows * tile) & (gx >= 0) & (gx < cols * tile)

    ext = ext_ref[...]
    n_ext = wide * line
    packed = ext
    for d in range(1, 3):
        packed = packed + pltpu.roll(pltpu.roll(ext, n_ext - d, 0), d * HEAD, 1)
    cat[...] = packed.astype(BF16)

    n_dec = (wide - 2) * line
    gain = gain_ref[...]
    half = n_dec // 2
    for part in range(2):
        lo = part * half
        acc = jnp.zeros((half, chan), F32)
        for dy in range(3):
            acc = acc + contract(
                cat[lo + dy * line : lo + dy * line + half, : 3 * HEAD], entry_ref[dy], 1, 0
            )
        value = acc.astype(BF16).astype(F32)
        dec[lo : lo + half] = value
        scaled = value * lax.rsqrt(jnp.mean(value * value, axis=1, keepdims=True) + NORM_EPS) * gain
        active = jnp.where(inside(2, lo, half), scaled * jax.nn.sigmoid(scaled), 0.0)
        hid[lo : lo + half, 0:chan] = active.astype(BF16)
    whole = hid[:, 0:chan].astype(F32)
    for d in range(1, 3):
        hid[:, d * chan : (d + 1) * chan] = pltpu.roll(whole, n_dec - d, 0).astype(BF16)

    n_ref = (wide - 4) * line
    tiles = 2
    step = n_ref // tiles
    rows_each = chan // tiles

    def residual(i, carry):
        lo = pl.multiple_of(i * step, 16)
        acc = jnp.zeros((step, chan), F32)
        for dy in range(3):
            acc = acc + contract(hid[pl.ds(pl.multiple_of(lo + dy * line, 16), step), :], res_ref[dy], 1, 0)
        center = pltpu.roll(dec[pl.ds(pl.multiple_of(lo + line, 8), step + 8), :], step + 7, 0)[:step]
        refined = (acc + center).astype(BF16).astype(F32)
        ref_[pl.ds(lo, step), :] = jnp.where(inside(1, lo, step), refined, 0.0)
        at = pl.ds(pl.multiple_of(i * rows_each, 16), rows_each)
        by_row = []
        for c in range(3):
            w = [up_ref[r, c, at, :].astype(F32) for r in range(3)]
            by_row.append((w[0], w[1] + w[2], w[0] + w[1], w[2]))
        for a in range(4):
            w = [by_row[c][a] for c in range(3)]
            for b, value in enumerate((w[0], w[1] + w[2], w[0] + w[1], w[2])):
                sums[a, b, at, :] = value.astype(BF16)
        return carry

    load_up.wait()
    lax.fori_loop(0, tiles, residual, 0)

    for y in range(tile + 2):
        for i in range(2):
            part = ref_[y * line + i * SLOT : y * line + (i + 1) * SLOT]
            for d in range(3):
                moved = part if d == 0 else pltpu.roll(part, SLOT - d, 0)
                shifted[d, (y * 2 + i) * tile : (y * 2 + i + 1) * tile, :] = moved[:tile].astype(BF16)

    count = tile * 2 * tile
    for a in range(2):
        for b in range(2):
            acc = jnp.zeros((count, chan), F32)
            for di in range(2):
                for dj in range(2):
                    lo = (a + di) * 2 * tile
                    acc = acc + contract(
                        shifted[b + dj, lo : lo + count, :], sums[2 * a + di, 2 * b + dj], 1, 0
                    )
            for n in range(chan // LANES):
                woven[n, pl.ds(b, count, stride=2), :] = acc[:, n * LANES : (n + 1) * LANES]
        for n in range(chan // LANES):
            value = woven[n].astype(BF16).reshape(tile, 2, 2 * tile, LANES)
            for i in range(2):
                out_ref[i, :, a, :, n * LANES : (n + 1) * LANES] = value[:, i]


def local(rows, cols, q, k, v, proj, entry, gain, res, up):
    images, tile, _, width = q.shape
    chan = res.shape[-1]
    tokens = tile * tile
    chips = rows * cols // 2
    blocks = -(-width // LANES)
    per_chip = -(-(2 * blocks + -(-blocks // 16)) // chips)
    wide = tile + 2 * HALO
    line = 2 * SLOT
    vmem = pl.BlockSpec(memory_space=pltpu.VMEM)
    hbm = pl.BlockSpec(memory_space=pltpu.HBM)
    flat = (images, tokens, width)
    unit = (16, LANES)
    dma = pltpu.SemaphoreType.DMA
    ext = pl.pallas_call(
        functools.partial(attention_kernel, rows, cols, tile, width, per_chip),
        out_shape=jax.ShapeDtypeStruct((wide * line, LANES), F32),
        in_specs=[hbm] * 4,
        out_specs=vmem,
        scratch_shapes=[
            pltpu.VMEM(flat, BF16), pltpu.VMEM(flat, BF16), pltpu.VMEM(flat, BF16),
            pltpu.VMEM((proj.shape[1], width), BF16),
            pltpu.VMEM((images, chips * per_chip) + unit, F32),
            pltpu.VMEM((chips * per_chip,) + unit, F32),
            pltpu.VMEM((chips, per_chip) + unit, BF16),
            pltpu.VMEM((chips, per_chip) + unit, BF16),
            pltpu.VMEM((images, chips, per_chip) + unit, BF16),
            pltpu.VMEM((images * tokens, LANES), F32),
            pltpu.VMEM((4, 2 * tile, LANES), BF16),
            pltpu.VMEM((8, 2 * tile, LANES), BF16),
            dma((6,)), dma((2,)), dma((chips,)), dma((chips,)), dma((chips,)), dma((chips,)),
            dma((8,)), dma((8,)), dma((chips,)), dma((chips,)),
        ],
        compiler_params=pltpu.CompilerParams(
            collective_id=0, has_side_effects=True, vmem_limit_bytes=24 * 1024 * 1024
        ),
        name="attention",
    )(*(pltpu.with_memory_space_constraint(x, pltpu.HBM) for x in (k.reshape(flat), v.reshape(flat), q.reshape(flat), proj.T)))
    count = tile * 2 * tile
    out = pl.pallas_call(
        functools.partial(decoder_kernel, rows, cols, tile),
        out_shape=jax.ShapeDtypeStruct((images, tile, 2, 2 * tile, chan), BF16),
        in_specs=[vmem] * 4 + [hbm],
        out_specs=vmem,
        scratch_shapes=[
            pltpu.VMEM(up.shape, BF16),
            pltpu.VMEM((wide * line, LANES), BF16),
            pltpu.VMEM(((wide - 2) * line, 3 * chan), BF16),
            pltpu.VMEM(((wide - 2) * line, chan), F32),
            pltpu.VMEM(((wide - 4) * line, chan), F32),
            pltpu.VMEM((3, (tile + 2) * 2 * tile, chan), BF16),
            pltpu.VMEM((4, 4, chan, chan), BF16),
            pltpu.VMEM((chan // LANES, 2 * count, LANES), F32),
            dma,
        ],
        compiler_params=pltpu.CompilerParams(vmem_limit_bytes=36 * 1024 * 1024),
        name="decoder",
    )(ext, entry.reshape(3, -1, chan), gain.reshape(1, chan), res.reshape(3, -1, chan), pltpu.with_memory_space_constraint(up, pltpu.HBM))
    return out.reshape(images, 2 * tile, 2 * tile, chan)


def solution(mesh):
    spread = P(None, "row", "col", None)
    rows, cols = mesh.shape["row"], mesh.shape["col"]
    return jax.shard_map(
        functools.partial(local, rows, cols),
        mesh=mesh,
        in_specs=(spread,) * 3 + (P(),) * 5,
        out_specs=spread,
        check_vma=False,
    )
```

```python
import functools

import jax
import jax.numpy as jnp
from jax import lax
from jax.experimental import pallas as pl
from jax.experimental.pallas import tpu as pltpu
from jax.sharding import PartitionSpec as P

HEAD = 32
NORM_EPS = 1e-06
LANES = 128
HALO = 3
SLOT = 24
MESH = pl.DeviceIdType.MESH
F32 = jnp.float32
BF16 = jnp.bfloat16
AROUND = ((-1, -1), (-1, 0), (-1, 1), (0, -1), (0, 1), (1, -1), (1, 0), (1, 1))


def contract(a, b, dim_a, dim_b):
    return lax.dot_general(a, b, (((dim_a,), (dim_b,)), ((), ())), preferred_element_type=F32)


def same_head(shape):
    return lax.broadcasted_iota(jnp.int32, shape, 0) // HEAD == lax.broadcasted_iota(
        jnp.int32, shape, 1
    ) // HEAD


def attention_kernel(
    rows, cols, tile, width, per_chip,
    k_hbm, v_hbm, q_hbm, proj_hbm, ext_ref,
    k_buf, v_buf, q_buf, proj, part, other, chip_sum, arrived, total, lat, strips, halo,
    in_sem, swap_sem, rs_send, rs_recv, ag_send, ag_recv, halo_send, halo_recv, fw_send, fw_recv,
):
    row, col = lax.axis_index("row"), lax.axis_index("col")
    core = lax.rem(col, 2)
    zs = cols // 2
    chips = rows * zs
    chip = row * zs + col // 2
    me = row * cols + col
    tokens = tile * tile
    blocks = -(-width // LANES)
    token_count = float(tokens * rows * cols)

    def place(c):
        return (c // zs, lax.rem(c, zs) * 2 + core)

    partner = (row, col + 1 - 2 * core)

    loads = {}
    for step in range(2):
        image = (1 - core) if step == 0 else core
        loads["k", step] = pltpu.make_async_copy(k_hbm.at[image], k_buf.at[image], in_sem.at[step])
        loads["v", step] = pltpu.make_async_copy(v_hbm.at[image], v_buf.at[image], in_sem.at[2 + step])
    load_proj = pltpu.make_async_copy(proj_hbm, proj, in_sem.at[4])
    load_q = pltpu.make_async_copy(q_hbm, q_buf, in_sem.at[5])
    for copy in loads.values():
        copy.start()
    load_proj.start()
    load_q.start()

    barrier = pltpu.get_barrier_semaphore()

    def greet(d, carry):
        t = lax.rem(me + d, rows * cols)
        pl.semaphore_signal(
            barrier, inc=1, device_id=(t // cols, lax.rem(t, cols)), device_id_type=MESH
        )
        return carry

    lax.fori_loop(1, rows * cols, greet, 0)

    span = -(-blocks // 2)
    groups = part.shape[2] // per_chip
    used = 1 + 2 * span
    part[:, :, 0:1] = jnp.zeros((2, 2, 1, 16, LANES), F32)
    if part.shape[2] > used:
        part[:, :, used:] = jnp.zeros((2, 2, part.shape[2] - used, 16, LANES), F32)
    mask = same_head((LANES, LANES))

    def of_half(half):
        return range(half * span, min((half + 1) * span, blocks))

    def sums(image, half):
        for n, b in enumerate(of_half(half)):
            lo = b * LANES
            w = min(LANES, width - lo)
            keys = jnp.maximum(k_buf[image, :, lo : lo + w], 0)
            values = v_buf[image, :, lo : lo + w]
            full = jnp.where(mask[:w, :w], contract(values, keys, 0, 0), 0.0)
            packed = full[0:HEAD]
            for h in range(1, w // HEAD):
                packed = packed + full[h * HEAD : (h + 1) * HEAD]
            mean = jnp.sum(keys.astype(F32), axis=0, keepdims=True)
            if w < LANES:
                packed = jnp.concatenate([packed, jnp.zeros((HEAD, LANES - w), F32)], axis=1)
            part[image, half, 1 + 2 * n] = packed[0:16]
            part[image, half, 2 + 2 * n] = packed[16:32]
            part[image, half, 0, n : n + 1, 0:w] = mean

    def swap(half):
        return pltpu.make_async_remote_copy(
            src_ref=part.at[1 - core, half], dst_ref=other.at[half], send_sem=swap_sem.at[half],
            recv_sem=swap_sem.at[2 + half], device_id=partner, device_id_type=MESH,
        )

    def each(first, last, body):
        def step(k, carry):
            body(k)
            return carry

        lax.fori_loop(first, last, step, 0)

    def scatter(half, k):
        g = lax.rem(chip // 2 + k, groups)
        t = 2 * g + half
        return t != chip, pltpu.make_async_remote_copy(
            src_ref=chip_sum.at[half, g], dst_ref=arrived.at[chip], send_sem=rs_send.at[t],
            recv_sem=rs_recv.at[chip], device_id=place(t), device_id_type=MESH,
        )

    def scatter_start(half, k):
        away, copy = scatter(half, k)
        pl.when(away)(copy.start)

    def scatter_end(half, k):
        away, copy = scatter(half, k)
        pl.when(away)(copy.wait_send)

    def owns(half):
        return (lax.rem(chip, 2) == half) & (chip // 2 < groups)

    def gather(half, k):
        t = lax.rem(chip + k, chips)
        mine = total.at[core, half, chip // 2]
        return pltpu.make_async_remote_copy(
            src_ref=mine, dst_ref=mine, send_sem=ag_send.at[k],
            recv_sem=ag_recv.at[chip], device_id=place(t), device_id_type=MESH,
        )

    def reduce(half):
        @pl.when(owns(half))
        def _():
            def add(k, acc):
                t = lax.rem(chip + k, chips)
                pltpu.make_async_remote_copy(
                    src_ref=arrived.at[t], dst_ref=arrived.at[t], send_sem=rs_send.at[t],
                    recv_sem=rs_recv.at[t], device_id=place(t), device_id_type=MESH,
                ).wait_recv()
                return acc + arrived[t].astype(F32)

            acc = lax.fori_loop(1, chips, add, chip_sum[half, chip // 2].astype(F32))
            total[core, half, chip // 2] = (acc / token_count).astype(BF16)
            each(1, chips, lambda k: gather(half, k).start())

    def collect(half):
        def one(g):
            t = 2 * g + half

            @pl.when(t != chip)
            def _():
                chunk = total.at[core, half, g]
                pltpu.make_async_remote_copy(
                    src_ref=chunk, dst_ref=chunk, send_sem=ag_send.at[0],
                    recv_sem=ag_recv.at[t], device_id=place(t), device_id_type=MESH,
                ).wait_recv()

        each(0, groups, one)
        forward(half).start()

    def forward(half):
        return pltpu.make_async_remote_copy(
            src_ref=total.at[core, half], dst_ref=total.at[core, half], send_sem=fw_send.at[half],
            recv_sem=fw_recv.at[half], device_id=partner, device_id_type=MESH,
        )

    def forwarded(half):
        theirs = total.at[1 - core, half]
        return pltpu.make_async_remote_copy(
            src_ref=theirs, dst_ref=theirs, send_sem=fw_send.at[half],
            recv_sem=fw_recv.at[half], device_id=partner, device_id_type=MESH,
        )

    loads["k", 0].wait()
    loads["v", 0].wait()
    sums(1 - core, 0)
    pl.semaphore_wait(barrier, rows * cols - 1)
    swap(0).start()
    loads["k", 1].wait()
    loads["v", 1].wait()
    for half in range(2):
        sums(core, half)
        if half == 0:
            sums(1 - core, 1)
            swap(1).start()
        swap(half).wait_recv()
        chip_sum[half] = (
            (part[core, half] + other[half]).reshape(chip_sum.shape[1:]).astype(BF16)
        )
        each(0, groups, functools.partial(scatter_start, half))
    for half in range(2):
        reduce(half)
    load_q.wait()
    load_proj.wait()

    def attend(image, half, state):
        squares, out = state

        def unit(u):
            return total[image, half, u // per_chip, u % per_chip].astype(F32)

        means = unit(0)
        for n, b in enumerate(of_half(half)):
            lo = b * LANES
            w = min(LANES, width - lo)
            packed = jnp.concatenate([unit(1 + 2 * n), unit(2 + 2 * n)], axis=0)
            spread = jnp.where(mask, jnp.concatenate([packed] * (LANES // HEAD), axis=0), 0.0)
            spread_mean = jnp.where(mask, jnp.broadcast_to(means[n : n + 1], (LANES, LANES)), 0.0)
            both = jnp.concatenate([spread, spread_mean], axis=0).astype(BF16)
            query = jnp.maximum(q_buf[image, :, lo : lo + w], 0)
            result = contract(query, both[:, :w], 1, 1)
            attended = result[:, :LANES] / jnp.maximum(result[:, LANES:], 1.0)
            squares = squares + attended * attended
            out = out + contract(attended[:, :w].astype(BF16), proj[:, lo : lo + w], 1, 1)
        return squares, out

    start = (jnp.zeros((tokens, LANES), F32), jnp.zeros((tokens, HEAD), F32))
    mine, theirs = start, start
    for half in range(2):
        collect(half)
        mine = attend(core, half, mine)
        forwarded(half).wait_recv()
        theirs = attend(1 - core, half, theirs)
    for image, (squares, out) in ((core, mine), (1 - core, theirs)):
        out = out * lax.rsqrt(jnp.sum(squares, axis=1, keepdims=True) / width + NORM_EPS)
        out = out.astype(BF16).astype(F32)
        lat[pl.ds(image * tokens, tokens)] = jnp.concatenate(
            [out, jnp.zeros((tokens, LANES - HEAD), F32)], axis=1
        )

    ext_ref[...] = jnp.zeros(ext_ref.shape, F32)
    line = 2 * SLOT

    def pack(pieces):
        packed = pieces[0]
        for i in range(1, HALO):
            packed = packed + pltpu.roll(pieces[i], i * HEAD, 1)
        return packed.astype(BF16)

    def rows_of(first):
        return pack([
            jnp.concatenate(
                [lat[i * tokens + (first + r) * tile : i * tokens + (first + r + 1) * tile] for i in range(2)],
                axis=0,
            )
            for r in range(HALO)
        ])

    def cols_of(first):
        return pack([lat[pl.ds(first + c, 2 * tile, stride=tile)] for c in range(HALO)])

    strips[0] = rows_of(0)
    strips[1] = rows_of(tile - HALO)
    strips[2] = cols_of(0)
    strips[3] = cols_of(tile - HALO)

    def exchange(d):
        dr, dc = AROUND[d]
        source = (0 if dr < 0 else 1) if dr else (2 if dc < 0 else 3)
        there = (
            (row + dr >= 0) & (row + dr < rows) & (col + dc >= 0) & (col + dc < cols)
        )
        return there, pltpu.make_async_remote_copy(
            src_ref=strips.at[source], dst_ref=halo.at[7 - d], send_sem=halo_send.at[d],
            recv_sem=halo_recv.at[7 - d], device_id=(row + dr, col + dc), device_id_type=MESH,
        )

    def exchange_from(d):
        dr, dc = AROUND[d]
        there = (
            (row + dr >= 0) & (row + dr < rows) & (col + dc >= 0) & (col + dc < cols)
        )
        return there, pltpu.make_async_remote_copy(
            src_ref=strips.at[0], dst_ref=halo.at[d], send_sem=halo_send.at[d],
            recv_sem=halo_recv.at[d], device_id=(row + dr, col + dc), device_id_type=MESH,
        )

    for d in range(8):
        there, copy = exchange(d)
        pl.when(there)(copy.start)

    for i in range(2):
        for y in range(tile):
            ext_ref[pl.ds((y + HALO) * line + i * SLOT + HALO, tile)] = lat[
                i * tokens + y * tile : i * tokens + (y + 1) * tile
            ]

    lane = lax.broadcasted_iota(jnp.int32, (2 * tile, LANES), 1)

    def take(d):
        dr, dc = AROUND[d]
        packed = halo[d].astype(F32)
        for n in range(HALO):
            piece = packed if n == 0 else pltpu.roll(packed, LANES - n * HEAD, 1)
            piece = jnp.where(lane < HEAD, piece, 0.0)
            for i in range(2):
                one = piece[i * tile : (i + 1) * tile]
                if dr:
                    y = n if dr < 0 else HALO + tile + n
                    at = y * line + i * SLOT
                    if dc < 0:
                        ext_ref[pl.ds(at, HALO)] = one[tile - HALO :]
                    elif dc == 0:
                        ext_ref[pl.ds(at + HALO, tile)] = one
                    else:
                        ext_ref[pl.ds(at + HALO + tile, HALO)] = one[:HALO]
                else:
                    x = n if dc < 0 else HALO + tile + n
                    ext_ref[pl.ds(HALO * line + i * SLOT + x, tile, stride=line)] = one

    for d in range(8):
        there, copy = exchange_from(d)

        @pl.when(there)
        def _(copy=copy, d=d):
            copy.wait_recv()
            take(d)

    for half in range(2):
        swap(half).wait_send()
        forward(half).wait_send()
        each(0, groups, functools.partial(scatter_end, half))
        pl.when(owns(half))(
            lambda half=half: each(1, chips, lambda k: gather(half, k).wait_send())
        )
    for d in range(8):
        there, copy = exchange(d)
        pl.when(there)(copy.wait_send)


def decoder_kernel(
    rows, cols, tile, ext_ref, entry_ref, gain_ref, res_ref, up_hbm, out_ref,
    up_ref, cat, hid, dec, ref_, shifted, sums, woven, up_sem,
):
    load_up = pltpu.make_async_copy(up_hbm, up_ref, up_sem)
    load_up.start()
    row, col = lax.axis_index("row"), lax.axis_index("col")
    line = 2 * SLOT
    wide = tile + 2 * HALO
    chan = res_ref.shape[-1]

    def inside(reach, first, count):
        p = first + lax.broadcasted_iota(jnp.int32, (count, 1), 0)
        y, x = p // line - reach, lax.rem(lax.rem(p, line), SLOT) - reach
        gy, gx = row * tile + y, col * tile + x
        return (gy >= 0) & (gy < rows * tile) & (gx >= 0) & (gx < cols * tile)

    ext = ext_ref[...]
    n_ext = wide * line
    packed = ext
    for d in range(1, 3):
        packed = packed + pltpu.roll(pltpu.roll(ext, n_ext - d, 0), d * HEAD, 1)
    cat[...] = packed.astype(BF16)

    n_dec = (wide - 2) * line
    gain = gain_ref[...]
    half = n_dec // 2
    for part in range(2):
        lo = part * half
        acc = jnp.zeros((half, chan), F32)
        for dy in range(3):
            acc = acc + contract(
                cat[lo + dy * line : lo + dy * line + half, : 3 * HEAD], entry_ref[dy], 1, 0
            )
        value = acc.astype(BF16).astype(F32)
        dec[lo : lo + half] = value
        scaled = value * lax.rsqrt(jnp.mean(value * value, axis=1, keepdims=True) + NORM_EPS) * gain
        active = jnp.where(inside(2, lo, half), scaled * jax.nn.sigmoid(scaled), 0.0)
        hid[lo : lo + half, 0:chan] = active.astype(BF16)
    whole = hid[:, 0:chan].astype(F32)
    for d in range(1, 3):
        hid[:, d * chan : (d + 1) * chan] = pltpu.roll(whole, n_dec - d, 0).astype(BF16)

    n_ref = (wide - 4) * line
    tiles = 2
    step = n_ref // tiles

    def residual(i):
        lo = i * step
        acc = jnp.zeros((step, chan), F32)
        for dy in range(3):
            acc = acc + contract(hid[pl.ds(lo + dy * line, step), :], res_ref[dy], 1, 0)
        center = pltpu.roll(dec[pl.ds(lo + line, step + 8), :], step + 7, 0)[:step]
        refined = (acc + center).astype(BF16).astype(F32)
        ref_[pl.ds(lo, step), :] = jnp.where(inside(1, lo, step), refined, 0.0)

    residual(0)
    load_up.wait()
    by_row = []
    for c in range(3):
        w = [up_ref[r, c].astype(F32) for r in range(3)]
        by_row.append((w[0], w[1] + w[2], w[0] + w[1], w[2]))
    for a in range(4):
        w = [by_row[c][a] for c in range(3)]
        for b, value in enumerate((w[0], w[1] + w[2], w[0] + w[1], w[2])):
            sums[a, b] = value.astype(BF16)
    residual(1)

    for y in range(tile + 2):
        for i in range(2):
            part = ref_[y * line + i * SLOT : y * line + (i + 1) * SLOT]
            for d in range(3):
                moved = part if d == 0 else pltpu.roll(part, SLOT - d, 0)
                shifted[d, (y * 2 + i) * tile : (y * 2 + i + 1) * tile, :] = moved[:tile].astype(BF16)

    count = tile * 2 * tile
    for a in range(2):
        for b in range(2):
            acc = jnp.zeros((count, chan), F32)
            for di in range(2):
                for dj in range(2):
                    lo = (a + di) * 2 * tile
                    acc = acc + contract(
                        shifted[b + dj, lo : lo + count, :], sums[2 * a + di, 2 * b + dj], 1, 0
                    )
            for n in range(chan // LANES):
                woven[n, pl.ds(b, count, stride=2), :] = acc[:, n * LANES : (n + 1) * LANES]
        for n in range(chan // LANES):
            value = woven[n].astype(BF16).reshape(tile, 2, 2 * tile, LANES)
            for i in range(2):
                out_ref[i, :, a, :, n * LANES : (n + 1) * LANES] = value[:, i]


def local(rows, cols, q, k, v, proj, entry, gain, res, up):
    images, tile, _, width = q.shape
    chan = res.shape[-1]
    tokens = tile * tile
    chips = rows * cols // 2
    blocks = -(-width // LANES)
    span = -(-blocks // 2)
    per_chip = -(-(1 + 2 * span) // (chips // 2))
    groups = -(-(1 + 2 * span) // per_chip)
    wide = tile + 2 * HALO
    line = 2 * SLOT
    vmem = pl.BlockSpec(memory_space=pltpu.VMEM)
    hbm = pl.BlockSpec(memory_space=pltpu.HBM)
    flat = (images, tokens, width)
    unit = (16, LANES)
    dma = pltpu.SemaphoreType.DMA
    ext = pl.pallas_call(
        functools.partial(attention_kernel, rows, cols, tile, width, per_chip),
        out_shape=jax.ShapeDtypeStruct((wide * line, LANES), F32),
        in_specs=[hbm] * 4,
        out_specs=vmem,
        scratch_shapes=[
            pltpu.VMEM(flat, BF16), pltpu.VMEM(flat, BF16), pltpu.VMEM(flat, BF16),
            pltpu.VMEM((proj.shape[1], width), BF16),
            pltpu.VMEM((images, 2, groups * per_chip) + unit, F32),
            pltpu.VMEM((2, groups * per_chip) + unit, F32),
            pltpu.VMEM((2, groups, per_chip) + unit, BF16),
            pltpu.VMEM((chips, per_chip) + unit, BF16),
            pltpu.VMEM((images, 2, groups, per_chip) + unit, BF16),
            pltpu.VMEM((images * tokens, LANES), F32),
            pltpu.VMEM((4, 2 * tile, LANES), BF16),
            pltpu.VMEM((8, 2 * tile, LANES), BF16),
            dma((6,)), dma((4,)), dma((chips,)), dma((chips,)), dma((chips,)), dma((chips,)),
            dma((8,)), dma((8,)), dma((2,)), dma((2,)),
        ],
        compiler_params=pltpu.CompilerParams(
            collective_id=0, has_side_effects=True, vmem_limit_bytes=24 * 1024 * 1024
        ),
        name="attention",
    )(*(pltpu.with_memory_space_constraint(x, pltpu.HBM) for x in (k.reshape(flat), v.reshape(flat), q.reshape(flat), proj.T)))
    count = tile * 2 * tile
    out = pl.pallas_call(
        functools.partial(decoder_kernel, rows, cols, tile),
        out_shape=jax.ShapeDtypeStruct((images, tile, 2, 2 * tile, chan), BF16),
        in_specs=[vmem] * 4 + [hbm],
        out_specs=vmem,
        scratch_shapes=[
            pltpu.VMEM(up.shape, BF16),
            pltpu.VMEM((wide * line, LANES), BF16),
            pltpu.VMEM(((wide - 2) * line, 3 * chan), BF16),
            pltpu.VMEM(((wide - 2) * line, chan), F32),
            pltpu.VMEM(((wide - 4) * line, chan), F32),
            pltpu.VMEM((3, (tile + 2) * 2 * tile, chan), BF16),
            pltpu.VMEM((4, 4, chan, chan), BF16),
            pltpu.VMEM((chan // LANES, 2 * count, LANES), F32),
            dma,
        ],
        compiler_params=pltpu.CompilerParams(vmem_limit_bytes=36 * 1024 * 1024),
        name="decoder",
    )(ext, entry.reshape(3, -1, chan), gain.reshape(1, chan), res.reshape(3, -1, chan), pltpu.with_memory_space_constraint(up, pltpu.HBM))
    return out.reshape(images, 2 * tile, 2 * tile, chan)


def solution(mesh):
    spread = P(None, "row", "col", None)
    rows, cols = mesh.shape["row"], mesh.shape["col"]
    return jax.shard_map(
        functools.partial(local, rows, cols),
        mesh=mesh,
        in_specs=(spread,) * 3 + (P(),) * 5,
        out_specs=spread,
        check_vma=False,
    )
```

```python
import functools

import jax
import jax.numpy as jnp
from jax import lax
from jax.experimental import pallas as pl
from jax.experimental.pallas import tpu as pltpu
from jax.sharding import PartitionSpec as P

HEAD = 32
NORM_EPS = 1e-06
LANES = 128
HALO = 3
SLOT = 24
MESH = pl.DeviceIdType.MESH
F32 = jnp.float32
BF16 = jnp.bfloat16
AROUND = ((-1, -1), (-1, 0), (-1, 1), (0, -1), (0, 1), (1, -1), (1, 0), (1, 1))


def contract(a, b, dim_a, dim_b):
    return lax.dot_general(a, b, (((dim_a,), (dim_b,)), ((), ())), preferred_element_type=F32)


def same_head(shape):
    return lax.broadcasted_iota(jnp.int32, shape, 0) // HEAD == lax.broadcasted_iota(
        jnp.int32, shape, 1
    ) // HEAD


def attention_kernel(
    rows, cols, tile, width, per_chip,
    k_hbm, v_hbm, q_hbm, proj_hbm, ext_ref,
    k_buf, v_buf, q_buf, proj, part, other, chip_sum, arrived, total, lat, strips, halo,
    in_sem, swap_sem, rs_send, rs_recv, ag_send, ag_recv, halo_send, halo_recv, fw_send, fw_recv,
):
    row, col = lax.axis_index("row"), lax.axis_index("col")
    core = lax.rem(col, 2)
    zs = cols // 2
    chips = rows * zs
    chip = row * zs + col // 2
    me = row * cols + col
    tokens = tile * tile
    blocks = -(-width // LANES)
    token_count = float(tokens * rows * cols)

    def place(c):
        return (c // zs, lax.rem(c, zs) * 2 + core)

    partner = (row, col + 1 - 2 * core)

    loads = {}
    for step in range(2):
        image = (1 - core) if step == 0 else core
        loads["k", step] = pltpu.make_async_copy(k_hbm.at[image], k_buf.at[image], in_sem.at[step])
        loads["v", step] = pltpu.make_async_copy(v_hbm.at[image], v_buf.at[image], in_sem.at[2 + step])
    load_proj = pltpu.make_async_copy(proj_hbm, proj, in_sem.at[4])
    load_q = pltpu.make_async_copy(q_hbm, q_buf, in_sem.at[5])
    for copy in loads.values():
        copy.start()
    load_proj.start()
    load_q.start()

    barrier = pltpu.get_barrier_semaphore()

    def greet(d, carry):
        t = lax.rem(me + d, rows * cols)
        pl.semaphore_signal(
            barrier, inc=1, device_id=(t // cols, lax.rem(t, cols)), device_id_type=MESH
        )
        return carry

    lax.fori_loop(1, rows * cols, greet, 0)

    span = -(-blocks // 2)
    groups = part.shape[2] // per_chip
    used = 1 + 2 * span
    part[:, :, 0:1] = jnp.zeros((2, 2, 1, 16, LANES), F32)
    if part.shape[2] > used:
        part[:, :, used:] = jnp.zeros((2, 2, part.shape[2] - used, 16, LANES), F32)
    mask = same_head((LANES, LANES))

    def of_half(half):
        return range(half * span, min((half + 1) * span, blocks))

    def sums(image, half):
        for n, b in enumerate(of_half(half)):
            lo = b * LANES
            w = min(LANES, width - lo)
            keys = jnp.maximum(k_buf[image, :, lo : lo + w], 0)
            values = v_buf[image, :, lo : lo + w]
            full = jnp.where(mask[:w, :w], contract(values, keys, 0, 0), 0.0)
            packed = full[0:HEAD]
            for h in range(1, w // HEAD):
                packed = packed + full[h * HEAD : (h + 1) * HEAD]
            mean = jnp.sum(keys.astype(F32), axis=0, keepdims=True)
            if w < LANES:
                packed = jnp.concatenate([packed, jnp.zeros((HEAD, LANES - w), F32)], axis=1)
            part[image, half, 1 + 2 * n] = packed[0:16]
            part[image, half, 2 + 2 * n] = packed[16:32]
            part[image, half, 0, n : n + 1, 0:w] = mean

    def swap(half):
        return pltpu.make_async_remote_copy(
            src_ref=part.at[1 - core, half], dst_ref=other.at[half], send_sem=swap_sem.at[half],
            recv_sem=swap_sem.at[2 + half], device_id=partner, device_id_type=MESH,
        )

    def each(first, last, body):
        def step(k, carry):
            body(k)
            return carry

        lax.fori_loop(first, last, step, 0)

    def scatter(half, k):
        g = lax.rem(chip // 2 + k, groups)
        t = 2 * g + half
        return t != chip, pltpu.make_async_remote_copy(
            src_ref=chip_sum.at[half, g], dst_ref=arrived.at[chip], send_sem=rs_send.at[t],
            recv_sem=rs_recv.at[chip], device_id=place(t), device_id_type=MESH,
        )

    def scatter_start(half, k):
        away, copy = scatter(half, k)
        pl.when(away)(copy.start)

    def scatter_end(half, k):
        away, copy = scatter(half, k)
        pl.when(away)(copy.wait_send)

    def owns(half):
        return (lax.rem(chip, 2) == half) & (chip // 2 < groups)

    def gather(half, k):
        t = lax.rem(chip + k, chips)
        mine = total.at[core, half, chip // 2]
        return pltpu.make_async_remote_copy(
            src_ref=mine, dst_ref=mine, send_sem=ag_send.at[k],
            recv_sem=ag_recv.at[chip], device_id=place(t), device_id_type=MESH,
        )

    def reduce(half):
        @pl.when(owns(half))
        def _():
            def add(k, acc):
                t = lax.rem(chip + k, chips)
                pltpu.make_async_remote_copy(
                    src_ref=arrived.at[t], dst_ref=arrived.at[t], send_sem=rs_send.at[t],
                    recv_sem=rs_recv.at[t], device_id=place(t), device_id_type=MESH,
                ).wait_recv()
                return acc + arrived[t].astype(F32)

            acc = lax.fori_loop(1, chips, add, chip_sum[half, chip // 2].astype(F32))
            total[core, half, chip // 2] = (acc / token_count).astype(BF16)
            each(1, chips, lambda k: gather(half, k).start())

    def collect(half):
        def one(g):
            t = 2 * g + half

            @pl.when(t != chip)
            def _():
                chunk = total.at[core, half, g]
                pltpu.make_async_remote_copy(
                    src_ref=chunk, dst_ref=chunk, send_sem=ag_send.at[0],
                    recv_sem=ag_recv.at[t], device_id=place(t), device_id_type=MESH,
                ).wait_recv()

        each(0, groups, one)
        forward(half).start()

    def forward(half):
        return pltpu.make_async_remote_copy(
            src_ref=total.at[core, half], dst_ref=total.at[core, half], send_sem=fw_send.at[half],
            recv_sem=fw_recv.at[half], device_id=partner, device_id_type=MESH,
        )

    def forwarded(half):
        theirs = total.at[1 - core, half]
        return pltpu.make_async_remote_copy(
            src_ref=theirs, dst_ref=theirs, send_sem=fw_send.at[half],
            recv_sem=fw_recv.at[half], device_id=partner, device_id_type=MESH,
        )

    loads["k", 0].wait()
    loads["v", 0].wait()
    sums(1 - core, 0)
    pl.semaphore_wait(barrier, rows * cols - 1)
    swap(0).start()
    loads["k", 1].wait()
    loads["v", 1].wait()
    for half in range(2):
        if half == 1:
            sums(1 - core, 1)
            swap(1).start()
        sums(core, half)
        swap(half).wait_recv()
        chip_sum[half] = (
            (part[core, half] + other[half]).reshape(chip_sum.shape[1:]).astype(BF16)
        )
        each(0, groups, functools.partial(scatter_start, half))
    for half in range(2):
        reduce(half)
    load_q.wait()
    load_proj.wait()

    def attend(image, half, state):
        squares, out = state

        def unit(u):
            return total[image, half, u // per_chip, u % per_chip].astype(F32)

        means = unit(0)
        for n, b in enumerate(of_half(half)):
            lo = b * LANES
            w = min(LANES, width - lo)
            packed = jnp.concatenate([unit(1 + 2 * n), unit(2 + 2 * n)], axis=0)
            spread = jnp.where(mask, jnp.concatenate([packed] * (LANES // HEAD), axis=0), 0.0)
            spread_mean = jnp.where(mask, jnp.broadcast_to(means[n : n + 1], (LANES, LANES)), 0.0)
            both = jnp.concatenate([spread, spread_mean], axis=0).astype(BF16)
            query = jnp.maximum(q_buf[image, :, lo : lo + w], 0)
            result = contract(query, both[:, :w], 1, 1)
            attended = result[:, :LANES] / jnp.maximum(result[:, LANES:], 1.0)
            squares = squares + attended * attended
            out = out + contract(attended[:, :w].astype(BF16), proj[:, lo : lo + w], 1, 1)
        return squares, out

    start = (jnp.zeros((tokens, LANES), F32), jnp.zeros((tokens, HEAD), F32))
    mine, theirs = start, start
    for half in range(2):
        collect(half)
        mine = attend(core, half, mine)
        forwarded(half).wait_recv()
        theirs = attend(1 - core, half, theirs)
    for image, (squares, out) in ((core, mine), (1 - core, theirs)):
        out = out * lax.rsqrt(jnp.sum(squares, axis=1, keepdims=True) / width + NORM_EPS)
        out = out.astype(BF16).astype(F32)
        lat[pl.ds(image * tokens, tokens)] = jnp.concatenate(
            [out, jnp.zeros((tokens, LANES - HEAD), F32)], axis=1
        )

    ext_ref[...] = jnp.zeros(ext_ref.shape, F32)
    line = 2 * SLOT

    def pack(pieces):
        packed = pieces[0]
        for i in range(1, HALO):
            packed = packed + pltpu.roll(pieces[i], i * HEAD, 1)
        return packed.astype(BF16)

    def rows_of(first):
        return pack([
            jnp.concatenate(
                [lat[i * tokens + (first + r) * tile : i * tokens + (first + r + 1) * tile] for i in range(2)],
                axis=0,
            )
            for r in range(HALO)
        ])

    def cols_of(first):
        return pack([lat[pl.ds(first + c, 2 * tile, stride=tile)] for c in range(HALO)])

    strips[0] = rows_of(0)
    strips[1] = rows_of(tile - HALO)
    strips[2] = cols_of(0)
    strips[3] = cols_of(tile - HALO)

    def exchange(d):
        dr, dc = AROUND[d]
        source = (0 if dr < 0 else 1) if dr else (2 if dc < 0 else 3)
        there = (
            (row + dr >= 0) & (row + dr < rows) & (col + dc >= 0) & (col + dc < cols)
        )
        return there, pltpu.make_async_remote_copy(
            src_ref=strips.at[source], dst_ref=halo.at[7 - d], send_sem=halo_send.at[d],
            recv_sem=halo_recv.at[7 - d], device_id=(row + dr, col + dc), device_id_type=MESH,
        )

    def exchange_from(d):
        dr, dc = AROUND[d]
        there = (
            (row + dr >= 0) & (row + dr < rows) & (col + dc >= 0) & (col + dc < cols)
        )
        return there, pltpu.make_async_remote_copy(
            src_ref=strips.at[0], dst_ref=halo.at[d], send_sem=halo_send.at[d],
            recv_sem=halo_recv.at[d], device_id=(row + dr, col + dc), device_id_type=MESH,
        )

    for d in range(8):
        there, copy = exchange(d)
        pl.when(there)(copy.start)

    for i in range(2):
        for y in range(tile):
            ext_ref[pl.ds((y + HALO) * line + i * SLOT + HALO, tile)] = lat[
                i * tokens + y * tile : i * tokens + (y + 1) * tile
            ]

    lane = lax.broadcasted_iota(jnp.int32, (2 * tile, LANES), 1)

    def take(d):
        dr, dc = AROUND[d]
        packed = halo[d].astype(F32)
        for n in range(HALO):
            piece = packed if n == 0 else pltpu.roll(packed, LANES - n * HEAD, 1)
            piece = jnp.where(lane < HEAD, piece, 0.0)
            for i in range(2):
                one = piece[i * tile : (i + 1) * tile]
                if dr:
                    y = n if dr < 0 else HALO + tile + n
                    at = y * line + i * SLOT
                    if dc < 0:
                        ext_ref[pl.ds(at, HALO)] = one[tile - HALO :]
                    elif dc == 0:
                        ext_ref[pl.ds(at + HALO, tile)] = one
                    else:
                        ext_ref[pl.ds(at + HALO + tile, HALO)] = one[:HALO]
                else:
                    x = n if dc < 0 else HALO + tile + n
                    ext_ref[pl.ds(HALO * line + i * SLOT + x, tile, stride=line)] = one

    for d in range(8):
        there, copy = exchange_from(d)

        @pl.when(there)
        def _(copy=copy, d=d):
            copy.wait_recv()
            take(d)

    for half in range(2):
        swap(half).wait_send()
        forward(half).wait_send()
        each(0, groups, functools.partial(scatter_end, half))
        pl.when(owns(half))(
            lambda half=half: each(1, chips, lambda k: gather(half, k).wait_send())
        )
    for d in range(8):
        there, copy = exchange(d)
        pl.when(there)(copy.wait_send)


def decoder_kernel(
    rows, cols, tile, ext_ref, entry_ref, gain_ref, res_ref, up_hbm, out_ref,
    up_ref, cat, hid, dec, ref_, shifted, sums, woven, out_buf, up_sem, out_sem,
):
    load_up = pltpu.make_async_copy(up_hbm, up_ref, up_sem)
    load_up.start()
    row, col = lax.axis_index("row"), lax.axis_index("col")
    line = 2 * SLOT
    wide = tile + 2 * HALO
    chan = res_ref.shape[-1]

    def inside(reach, first, count):
        p = first + lax.broadcasted_iota(jnp.int32, (count, 1), 0)
        y, x = p // line - reach, lax.rem(lax.rem(p, line), SLOT) - reach
        gy, gx = row * tile + y, col * tile + x
        return (gy >= 0) & (gy < rows * tile) & (gx >= 0) & (gx < cols * tile)

    ext = ext_ref[...]
    n_ext = wide * line
    packed = ext
    for d in range(1, 3):
        packed = packed + pltpu.roll(pltpu.roll(ext, n_ext - d, 0), d * HEAD, 1)
    cat[...] = packed.astype(BF16)

    n_dec = (wide - 2) * line
    gain = gain_ref[...]
    half = n_dec // 2
    for part in range(2):
        lo = part * half
        acc = jnp.zeros((half, chan), F32)
        for dy in range(3):
            acc = acc + contract(
                cat[lo + dy * line : lo + dy * line + half, : 3 * HEAD], entry_ref[dy], 1, 0
            )
        value = acc.astype(BF16).astype(F32)
        dec[lo : lo + half] = value
        scaled = value * lax.rsqrt(jnp.mean(value * value, axis=1, keepdims=True) + NORM_EPS) * gain
        active = jnp.where(inside(2, lo, half), scaled * jax.nn.sigmoid(scaled), 0.0)
        hid[lo : lo + half, 0:chan] = active.astype(BF16)
    whole = hid[:, 0:chan].astype(F32)
    for d in range(1, 3):
        hid[:, d * chan : (d + 1) * chan] = pltpu.roll(whole, n_dec - d, 0).astype(BF16)

    n_ref = (wide - 4) * line
    tiles = 2
    step = n_ref // tiles

    def residual(i):
        lo = i * step
        acc = jnp.zeros((step, chan), F32)
        for dy in range(3):
            acc = acc + contract(hid[pl.ds(lo + dy * line, step), :], res_ref[dy], 1, 0)
        center = pltpu.roll(dec[pl.ds(lo + line, step + 8), :], step + 7, 0)[:step]
        refined = (acc + center).astype(BF16).astype(F32)
        ref_[pl.ds(lo, step), :] = jnp.where(inside(1, lo, step), refined, 0.0)

    residual(0)
    load_up.wait()
    taps = [[up_ref[r, c].astype(F32) for c in range(3)] for r in range(3)]
    down = [taps[0][c] + taps[1][c] + taps[2][c] for c in range(3)]
    sums[0] = (down[0] + down[1] + down[2]).astype(BF16)
    for n in range(2):
        sums[1 + n] = down[2 * n].astype(BF16)
        sums[3 + n] = (taps[2 * n][0] + taps[2 * n][1] + taps[2 * n][2]).astype(BF16)
    residual(1)

    for y in range(tile + 2):
        for i in range(2):
            part = ref_[y * line + i * SLOT : y * line + (i + 1) * SLOT]
            center = pltpu.roll(part, SLOT - 1, 0)[:tile]
            after = pltpu.roll(part, SLOT - 2, 0)[:tile]
            at = slice((y * 2 + i) * tile, (y * 2 + i + 1) * tile)
            shifted[0, at, :] = (part[:tile] - center).astype(BF16)
            shifted[1, at, :] = center.astype(BF16)
            shifted[2, at, :] = (after - center).astype(BF16)

    count = tile * 2 * tile
    mid = slice(2 * tile, 2 * tile + count)

    def row_step(field, a):
        lo = 4 * a * tile
        return (
            shifted[field, lo : lo + count, :].astype(F32) - shifted[field, mid, :].astype(F32)
        ).astype(BF16)

    base = contract(shifted[1, mid, :], sums[0], 1, 0)
    across = [base + contract(shifted[2 * b, mid, :], sums[1 + b], 1, 0) for b in range(2)]
    stores = []
    for a in range(2):
        along = contract(row_step(1, a), sums[3 + a], 1, 0)
        for b in range(2):
            acc = across[b] + along + contract(row_step(2 * b, a), up_ref[2 * a, 2 * b], 1, 0)
            for n in range(chan // LANES):
                woven[n, pl.ds(b, count, stride=2), :] = acc[:, n * LANES : (n + 1) * LANES]
        for n in range(chan // LANES):
            value = woven[n].astype(BF16).reshape(tile, 2, 2 * tile, LANES)
            for i in range(2):
                out_buf[a, i, :, :, n * LANES : (n + 1) * LANES] = value[:, i]
        stores.append(pltpu.make_async_copy(out_buf.at[a], out_ref.at[:, :, a], out_sem.at[a]))
        stores[-1].start()
    for store in stores:
        store.wait()


def local(rows, cols, q, k, v, proj, entry, gain, res, up):
    images, tile, _, width = q.shape
    chan = res.shape[-1]
    tokens = tile * tile
    chips = rows * cols // 2
    blocks = -(-width // LANES)
    span = -(-blocks // 2)
    per_chip = -(-(1 + 2 * span) // (chips // 2))
    groups = -(-(1 + 2 * span) // per_chip)
    wide = tile + 2 * HALO
    line = 2 * SLOT
    vmem = pl.BlockSpec(memory_space=pltpu.VMEM)
    hbm = pl.BlockSpec(memory_space=pltpu.HBM)
    flat = (images, tokens, width)
    unit = (16, LANES)
    dma = pltpu.SemaphoreType.DMA
    ext = pl.pallas_call(
        functools.partial(attention_kernel, rows, cols, tile, width, per_chip),
        out_shape=jax.ShapeDtypeStruct((wide * line, LANES), F32),
        in_specs=[hbm] * 4,
        out_specs=vmem,
        scratch_shapes=[
            pltpu.VMEM(flat, BF16), pltpu.VMEM(flat, BF16), pltpu.VMEM(flat, BF16),
            pltpu.VMEM((proj.shape[1], width), BF16),
            pltpu.VMEM((images, 2, groups * per_chip) + unit, F32),
            pltpu.VMEM((2, groups * per_chip) + unit, F32),
            pltpu.VMEM((2, groups, per_chip) + unit, BF16),
            pltpu.VMEM((chips, per_chip) + unit, BF16),
            pltpu.VMEM((images, 2, groups, per_chip) + unit, BF16),
            pltpu.VMEM((images * tokens, LANES), F32),
            pltpu.VMEM((4, 2 * tile, LANES), BF16),
            pltpu.VMEM((8, 2 * tile, LANES), BF16),
            dma((6,)), dma((4,)), dma((chips,)), dma((chips,)), dma((chips,)), dma((chips,)),
            dma((8,)), dma((8,)), dma((2,)), dma((2,)),
        ],
        compiler_params=pltpu.CompilerParams(
            collective_id=0, has_side_effects=True, vmem_limit_bytes=24 * 1024 * 1024
        ),
        name="attention",
    )(*(pltpu.with_memory_space_constraint(x, pltpu.HBM) for x in (k.reshape(flat), v.reshape(flat), q.reshape(flat), proj.T)))
    count = tile * 2 * tile
    out = pl.pallas_call(
        functools.partial(decoder_kernel, rows, cols, tile),
        out_shape=jax.ShapeDtypeStruct((images, tile, 2, 2 * tile, chan), BF16),
        in_specs=[vmem] * 4 + [hbm],
        out_specs=pl.BlockSpec(memory_space=pl.ANY),
        scratch_shapes=[
            pltpu.VMEM(up.shape, BF16),
            pltpu.VMEM((wide * line, LANES), BF16),
            pltpu.VMEM(((wide - 2) * line, 3 * chan), BF16),
            pltpu.VMEM(((wide - 2) * line, chan), F32),
            pltpu.VMEM(((wide - 4) * line, chan), F32),
            pltpu.VMEM((3, (tile + 2) * 2 * tile, chan), BF16),
            pltpu.VMEM((5, chan, chan), BF16),
            pltpu.VMEM((chan // LANES, 2 * count, LANES), F32),
            pltpu.VMEM((2, images, tile, 2 * tile, chan), BF16),
            dma,
            dma((2,)),
        ],
        compiler_params=pltpu.CompilerParams(vmem_limit_bytes=36 * 1024 * 1024),
        name="decoder",
    )(ext, entry.reshape(3, -1, chan), gain.reshape(1, chan), res.reshape(3, -1, chan), pltpu.with_memory_space_constraint(up, pltpu.HBM))
    return out.reshape(images, 2 * tile, 2 * tile, chan)


def solution(mesh):
    spread = P(None, "row", "col", None)
    rows, cols = mesh.shape["row"], mesh.shape["col"]
    return jax.shard_map(
        functools.partial(local, rows, cols),
        mesh=mesh,
        in_specs=(spread,) * 3 + (P(),) * 5,
        out_specs=spread,
        check_vma=False,
    )
```

```python
import functools

import jax
import jax.numpy as jnp
from jax import lax
from jax.experimental import pallas as pl
from jax.experimental.pallas import tpu as pltpu
from jax.sharding import PartitionSpec as P

HEAD = 32
NORM_EPS = 1e-06
LANES = 128
HALO = 3
SLOT = 24
MESH = pl.DeviceIdType.MESH
F32 = jnp.float32
BF16 = jnp.bfloat16
AROUND = ((-1, -1), (-1, 0), (-1, 1), (0, -1), (0, 1), (1, -1), (1, 0), (1, 1))


def contract(a, b, dim_a, dim_b):
    return lax.dot_general(a, b, (((dim_a,), (dim_b,)), ((), ())), preferred_element_type=F32)


def same_head(shape):
    return lax.broadcasted_iota(jnp.int32, shape, 0) // HEAD == lax.broadcasted_iota(
        jnp.int32, shape, 1
    ) // HEAD


def attention_kernel(
    rows, cols, tile, width, per_chip,
    k_hbm, v_hbm, q_hbm, proj_hbm, ext_ref,
    k_buf, v_buf, q_buf, proj, part, other, chip_sum, arrived, total, lat, strips, halo,
    in_sem, swap_sem, rs_send, rs_recv, ag_send, ag_recv, halo_send, halo_recv, fw_send, fw_recv,
):
    row, col = lax.axis_index("row"), lax.axis_index("col")
    core = lax.rem(col, 2)
    zs = cols // 2
    chips = rows * zs
    chip = row * zs + col // 2
    me = row * cols + col
    tokens = tile * tile
    blocks = -(-width // LANES)
    token_count = float(tokens * rows * cols)

    def place(c):
        return (c // zs, lax.rem(c, zs) * 2 + core)

    partner = (row, col + 1 - 2 * core)

    loads = {}
    for step in range(2):
        image = (1 - core) if step == 0 else core
        loads["k", step] = pltpu.make_async_copy(k_hbm.at[image], k_buf.at[image], in_sem.at[step])
        loads["v", step] = pltpu.make_async_copy(v_hbm.at[image], v_buf.at[image], in_sem.at[2 + step])
    load_proj = pltpu.make_async_copy(proj_hbm, proj, in_sem.at[4])
    load_q = pltpu.make_async_copy(q_hbm, q_buf, in_sem.at[5])
    for copy in loads.values():
        copy.start()

    barrier = pltpu.get_barrier_semaphore()

    def greet(d, carry):
        t = lax.rem(me + d, rows * cols)
        pl.semaphore_signal(
            barrier, inc=1, device_id=(t // cols, lax.rem(t, cols)), device_id_type=MESH
        )
        return carry

    lax.fori_loop(1, rows * cols, greet, 0)

    span = -(-blocks // 2)
    groups = part.shape[2] // per_chip
    used = 1 + 2 * span
    part[:, :, 0:1] = jnp.zeros((2, 2, 1, 16, LANES), F32)
    if part.shape[2] > used:
        part[:, :, used:] = jnp.zeros((2, 2, part.shape[2] - used, 16, LANES), F32)
    mask = same_head((LANES, LANES))

    def of_half(half):
        return range(half * span, min((half + 1) * span, blocks))

    def sums(image, half):
        for n, b in enumerate(of_half(half)):
            lo = b * LANES
            w = min(LANES, width - lo)
            keys = jnp.maximum(k_buf[image, :, lo : lo + w], 0)
            values = v_buf[image, :, lo : lo + w]
            full = jnp.where(mask[:w, :w], contract(values, keys, 0, 0), 0.0)
            packed = full[0:HEAD]
            for h in range(1, w // HEAD):
                packed = packed + full[h * HEAD : (h + 1) * HEAD]
            mean = jnp.sum(keys.astype(F32), axis=0, keepdims=True)
            if w < LANES:
                packed = jnp.concatenate([packed, jnp.zeros((HEAD, LANES - w), F32)], axis=1)
            part[image, half, 1 + 2 * n] = packed[0:16]
            part[image, half, 2 + 2 * n] = packed[16:32]
            part[image, half, 0, n : n + 1, 0:w] = mean

    def swap(half):
        return pltpu.make_async_remote_copy(
            src_ref=part.at[1 - core, half], dst_ref=other.at[half], send_sem=swap_sem.at[half],
            recv_sem=swap_sem.at[2 + half], device_id=partner, device_id_type=MESH,
        )

    def each(first, last, body):
        def step(k, carry):
            body(k)
            return carry

        lax.fori_loop(first, last, step, 0)

    def scatter(half, k):
        g = lax.rem(chip // 2 + k, groups)
        t = 2 * g + half
        return t != chip, pltpu.make_async_remote_copy(
            src_ref=chip_sum.at[half, g], dst_ref=arrived.at[chip], send_sem=rs_send.at[t],
            recv_sem=rs_recv.at[chip], device_id=place(t), device_id_type=MESH,
        )

    def scatter_start(half, k):
        away, copy = scatter(half, k)
        pl.when(away)(copy.start)

    def scatter_end(half, k):
        away, copy = scatter(half, k)
        pl.when(away)(copy.wait_send)

    def owns(half):
        return (lax.rem(chip, 2) == half) & (chip // 2 < groups)

    def gather(half, k):
        t = lax.rem(chip + k, chips)
        mine = total.at[core, half, chip // 2]
        return pltpu.make_async_remote_copy(
            src_ref=mine, dst_ref=mine, send_sem=ag_send.at[k],
            recv_sem=ag_recv.at[chip], device_id=place(t), device_id_type=MESH,
        )

    def reduce(half):
        @pl.when(owns(half))
        def _():
            def add(k, acc):
                t = lax.rem(chip + k, chips)
                pltpu.make_async_remote_copy(
                    src_ref=arrived.at[t], dst_ref=arrived.at[t], send_sem=rs_send.at[t],
                    recv_sem=rs_recv.at[t], device_id=place(t), device_id_type=MESH,
                ).wait_recv()
                return acc + arrived[t].astype(F32)

            acc = lax.fori_loop(1, chips, add, chip_sum[half, chip // 2].astype(F32))
            total[core, half, chip // 2] = (acc / token_count).astype(BF16)
            each(1, chips, lambda k: gather(half, k).start())

    def collect(half):
        def one(g):
            t = 2 * g + half

            @pl.when(t != chip)
            def _():
                chunk = total.at[core, half, g]
                pltpu.make_async_remote_copy(
                    src_ref=chunk, dst_ref=chunk, send_sem=ag_send.at[0],
                    recv_sem=ag_recv.at[t], device_id=place(t), device_id_type=MESH,
                ).wait_recv()

        each(0, groups, one)
        forward(half).start()

    def forward(half):
        return pltpu.make_async_remote_copy(
            src_ref=total.at[core, half], dst_ref=total.at[core, half], send_sem=fw_send.at[half],
            recv_sem=fw_recv.at[half], device_id=partner, device_id_type=MESH,
        )

    def forwarded(half):
        theirs = total.at[1 - core, half]
        return pltpu.make_async_remote_copy(
            src_ref=theirs, dst_ref=theirs, send_sem=fw_send.at[half],
            recv_sem=fw_recv.at[half], device_id=partner, device_id_type=MESH,
        )

    loads["k", 0].wait()
    loads["v", 0].wait()
    sums(1 - core, 0)
    pl.semaphore_wait(barrier, rows * cols - 1)
    swap(0).start()
    loads["k", 1].wait()
    loads["v", 1].wait()
    load_proj.start()
    load_q.start()
    for half in range(2):
        if half == 1:
            sums(1 - core, 1)
            swap(1).start()
        sums(core, half)
        swap(half).wait_recv()
        chip_sum[half] = (
            (part[core, half] + other[half]).reshape(chip_sum.shape[1:]).astype(BF16)
        )
        each(0, groups, functools.partial(scatter_start, half))
    for half in range(2):
        reduce(half)
    load_q.wait()
    load_proj.wait()

    def attend(image, half, state):
        squares, out = state

        def unit(u):
            return total[image, half, u // per_chip, u % per_chip].astype(F32)

        means = unit(0)
        for n, b in enumerate(of_half(half)):
            lo = b * LANES
            w = min(LANES, width - lo)
            packed = jnp.concatenate([unit(1 + 2 * n), unit(2 + 2 * n)], axis=0)
            spread = jnp.where(mask, jnp.concatenate([packed] * (LANES // HEAD), axis=0), 0.0)
            spread_mean = jnp.where(mask, jnp.broadcast_to(means[n : n + 1], (LANES, LANES)), 0.0)
            both = jnp.concatenate([spread, spread_mean], axis=0).astype(BF16)
            query = jnp.maximum(q_buf[image, :, lo : lo + w], 0)
            result = contract(query, both[:, :w], 1, 1)
            attended = result[:, :LANES] / jnp.maximum(result[:, LANES:], 1.0)
            squares = squares + attended * attended
            out = out + contract(attended[:, :w].astype(BF16), proj[:, lo : lo + w], 1, 1)
        return squares, out

    start = (jnp.zeros((tokens, LANES), F32), jnp.zeros((tokens, HEAD), F32))
    mine, theirs = start, start
    for half in range(2):
        collect(half)
        mine = attend(core, half, mine)
        forwarded(half).wait_recv()
        theirs = attend(1 - core, half, theirs)
    for image, (squares, out) in ((core, mine), (1 - core, theirs)):
        out = out * lax.rsqrt(jnp.sum(squares, axis=1, keepdims=True) / width + NORM_EPS)
        out = out.astype(BF16).astype(F32)
        lat[pl.ds(image * tokens, tokens)] = jnp.concatenate(
            [out, jnp.zeros((tokens, LANES - HEAD), F32)], axis=1
        )

    ext_ref[...] = jnp.zeros(ext_ref.shape, F32)
    line = 2 * SLOT

    def pack(pieces):
        packed = pieces[0]
        for i in range(1, HALO):
            packed = packed + pltpu.roll(pieces[i], i * HEAD, 1)
        return packed.astype(BF16)

    def rows_of(first):
        return pack([
            jnp.concatenate(
                [lat[i * tokens + (first + r) * tile : i * tokens + (first + r + 1) * tile] for i in range(2)],
                axis=0,
            )
            for r in range(HALO)
        ])

    def cols_of(first):
        return pack([lat[pl.ds(first + c, 2 * tile, stride=tile)] for c in range(HALO)])

    strips[0] = rows_of(0)
    strips[1] = rows_of(tile - HALO)
    strips[2] = cols_of(0)
    strips[3] = cols_of(tile - HALO)

    def exchange(d):
        dr, dc = AROUND[d]
        source = (0 if dr < 0 else 1) if dr else (2 if dc < 0 else 3)
        there = (
            (row + dr >= 0) & (row + dr < rows) & (col + dc >= 0) & (col + dc < cols)
        )
        return there, pltpu.make_async_remote_copy(
            src_ref=strips.at[source], dst_ref=halo.at[7 - d], send_sem=halo_send.at[d],
            recv_sem=halo_recv.at[7 - d], device_id=(row + dr, col + dc), device_id_type=MESH,
        )

    def exchange_from(d):
        dr, dc = AROUND[d]
        there = (
            (row + dr >= 0) & (row + dr < rows) & (col + dc >= 0) & (col + dc < cols)
        )
        return there, pltpu.make_async_remote_copy(
            src_ref=strips.at[0], dst_ref=halo.at[d], send_sem=halo_send.at[d],
            recv_sem=halo_recv.at[d], device_id=(row + dr, col + dc), device_id_type=MESH,
        )

    for d in range(8):
        there, copy = exchange(d)
        pl.when(there)(copy.start)

    for i in range(2):
        for y in range(tile):
            ext_ref[pl.ds((y + HALO) * line + i * SLOT + HALO, tile)] = lat[
                i * tokens + y * tile : i * tokens + (y + 1) * tile
            ]

    lane = lax.broadcasted_iota(jnp.int32, (2 * tile, LANES), 1)

    def take(d):
        dr, dc = AROUND[d]
        packed = halo[d].astype(F32)
        for n in range(HALO):
            piece = packed if n == 0 else pltpu.roll(packed, LANES - n * HEAD, 1)
            piece = jnp.where(lane < HEAD, piece, 0.0)
            for i in range(2):
                one = piece[i * tile : (i + 1) * tile]
                if dr:
                    y = n if dr < 0 else HALO + tile + n
                    at = y * line + i * SLOT
                    if dc < 0:
                        ext_ref[pl.ds(at, HALO)] = one[tile - HALO :]
                    elif dc == 0:
                        ext_ref[pl.ds(at + HALO, tile)] = one
                    else:
                        ext_ref[pl.ds(at + HALO + tile, HALO)] = one[:HALO]
                else:
                    x = n if dc < 0 else HALO + tile + n
                    ext_ref[pl.ds(HALO * line + i * SLOT + x, tile, stride=line)] = one

    for d in range(8):
        there, copy = exchange_from(d)

        @pl.when(there)
        def _(copy=copy, d=d):
            copy.wait_recv()
            take(d)

    for half in range(2):
        swap(half).wait_send()
        forward(half).wait_send()
        each(0, groups, functools.partial(scatter_end, half))
        pl.when(owns(half))(
            lambda half=half: each(1, chips, lambda k: gather(half, k).wait_send())
        )
    for d in range(8):
        there, copy = exchange(d)
        pl.when(there)(copy.wait_send)


def decoder_kernel(
    rows, cols, tile, ext_ref, entry_ref, gain_ref, res_ref, up_hbm, out_ref,
    up_ref, cat, hid, dec, ref_, shifted, sums, woven, out_buf, up_sem, out_sem,
):
    load_up = pltpu.make_async_copy(up_hbm, up_ref, up_sem)
    load_up.start()
    row, col = lax.axis_index("row"), lax.axis_index("col")
    line = 2 * SLOT
    wide = tile + 2 * HALO
    chan = res_ref.shape[-1]

    def inside(reach, first, count):
        p = first + lax.broadcasted_iota(jnp.int32, (count, 1), 0)
        y, x = p // line - reach, lax.rem(lax.rem(p, line), SLOT) - reach
        gy, gx = row * tile + y, col * tile + x
        return (gy >= 0) & (gy < rows * tile) & (gx >= 0) & (gx < cols * tile)

    ext = ext_ref[...]
    n_ext = wide * line
    packed = ext
    for d in range(1, 3):
        packed = packed + pltpu.roll(pltpu.roll(ext, n_ext - d, 0), d * HEAD, 1)
    cat[...] = packed.astype(BF16)

    n_dec = (wide - 2) * line
    gain = gain_ref[...]
    half = n_dec // 2
    for part in range(2):
        lo = part * half
        acc = jnp.zeros((half, chan), F32)
        for dy in range(3):
            acc = acc + contract(
                cat[lo + dy * line : lo + dy * line + half, : 3 * HEAD], entry_ref[dy], 1, 0
            )
        value = acc.astype(BF16).astype(F32)
        dec[lo : lo + half] = value
        scaled = value * lax.rsqrt(jnp.mean(value * value, axis=1, keepdims=True) + NORM_EPS) * gain
        active = jnp.where(inside(2, lo, half), scaled * jax.nn.sigmoid(scaled), 0.0)
        hid[lo : lo + half, 0:chan] = active.astype(BF16)
    whole = hid[:, 0:chan].astype(F32)
    for d in range(1, 3):
        hid[:, d * chan : (d + 1) * chan] = pltpu.roll(whole, n_dec - d, 0).astype(BF16)

    n_ref = (wide - 4) * line
    tiles = 2
    step = n_ref // tiles

    def residual(i):
        lo = i * step
        acc = jnp.zeros((step, chan), F32)
        for dy in range(3):
            acc = acc + contract(hid[pl.ds(lo + dy * line, step), :], res_ref[dy], 1, 0)
        center = pltpu.roll(dec[pl.ds(lo + line, step + 8), :], step + 7, 0)[:step]
        refined = (acc + center).astype(BF16).astype(F32)
        ref_[pl.ds(lo, step), :] = jnp.where(inside(1, lo, step), refined, 0.0)

    residual(0)
    load_up.wait()
    taps = [[up_ref[r, c].astype(F32) for c in range(3)] for r in range(3)]
    down = [taps[0][c] + taps[1][c] + taps[2][c] for c in range(3)]
    sums[0] = (down[0] + down[1] + down[2]).astype(BF16)
    for n in range(2):
        sums[1 + n] = down[2 * n].astype(BF16)
        sums[3 + n] = (taps[2 * n][0] + taps[2 * n][1] + taps[2 * n][2]).astype(BF16)
    residual(1)

    for y in range(tile + 2):
        for i in range(2):
            part = ref_[y * line + i * SLOT : y * line + (i + 1) * SLOT]
            center = pltpu.roll(part, SLOT - 1, 0)[:tile]
            after = pltpu.roll(part, SLOT - 2, 0)[:tile]
            at = slice((y * 2 + i) * tile, (y * 2 + i + 1) * tile)
            shifted[0, at, :] = (part[:tile] - center).astype(BF16)
            shifted[1, at, :] = center.astype(BF16)
            shifted[2, at, :] = (after - center).astype(BF16)

    count = tile * 2 * tile
    mid = slice(2 * tile, 2 * tile + count)

    def row_step(field, a):
        lo = 4 * a * tile
        return (
            shifted[field, lo : lo + count, :].astype(F32) - shifted[field, mid, :].astype(F32)
        ).astype(BF16)

    base = contract(shifted[1, mid, :], sums[0], 1, 0)
    across = [base + contract(shifted[2 * b, mid, :], sums[1 + b], 1, 0) for b in range(2)]
    stores = []
    for a in range(2):
        along = contract(row_step(1, a), sums[3 + a], 1, 0)
        for b in range(2):
            acc = across[b] + along + contract(row_step(2 * b, a), up_ref[2 * a, 2 * b], 1, 0)
            for n in range(chan // LANES):
                woven[n, pl.ds(b, count, stride=2), :] = acc[:, n * LANES : (n + 1) * LANES]
        for n in range(chan // LANES):
            value = woven[n].astype(BF16).reshape(tile, 2, 2 * tile, LANES)
            for i in range(2):
                out_buf[a, i, :, :, n * LANES : (n + 1) * LANES] = value[:, i]
        stores.append(pltpu.make_async_copy(out_buf.at[a], out_ref.at[:, :, a], out_sem.at[a]))
        stores[-1].start()
    for store in stores:
        store.wait()


def local(rows, cols, q, k, v, proj, entry, gain, res, up):
    images, tile, _, width = q.shape
    chan = res.shape[-1]
    tokens = tile * tile
    chips = rows * cols // 2
    blocks = -(-width // LANES)
    span = -(-blocks // 2)
    per_chip = -(-(1 + 2 * span) // (chips // 2))
    groups = -(-(1 + 2 * span) // per_chip)
    wide = tile + 2 * HALO
    line = 2 * SLOT
    vmem = pl.BlockSpec(memory_space=pltpu.VMEM)
    hbm = pl.BlockSpec(memory_space=pltpu.HBM)
    flat = (images, tokens, width)
    unit = (16, LANES)
    dma = pltpu.SemaphoreType.DMA
    ext = pl.pallas_call(
        functools.partial(attention_kernel, rows, cols, tile, width, per_chip),
        out_shape=jax.ShapeDtypeStruct((wide * line, LANES), F32),
        in_specs=[hbm] * 4,
        out_specs=vmem,
        scratch_shapes=[
            pltpu.VMEM(flat, BF16), pltpu.VMEM(flat, BF16), pltpu.VMEM(flat, BF16),
            pltpu.VMEM((proj.shape[1], width), BF16),
            pltpu.VMEM((images, 2, groups * per_chip) + unit, F32),
            pltpu.VMEM((2, groups * per_chip) + unit, F32),
            pltpu.VMEM((2, groups, per_chip) + unit, BF16),
            pltpu.VMEM((chips, per_chip) + unit, BF16),
            pltpu.VMEM((images, 2, groups, per_chip) + unit, BF16),
            pltpu.VMEM((images * tokens, LANES), F32),
            pltpu.VMEM((4, 2 * tile, LANES), BF16),
            pltpu.VMEM((8, 2 * tile, LANES), BF16),
            dma((6,)), dma((4,)), dma((chips,)), dma((chips,)), dma((chips,)), dma((chips,)),
            dma((8,)), dma((8,)), dma((2,)), dma((2,)),
        ],
        compiler_params=pltpu.CompilerParams(
            collective_id=0, has_side_effects=True, vmem_limit_bytes=24 * 1024 * 1024
        ),
        name="attention",
    )(*(pltpu.with_memory_space_constraint(x, pltpu.HBM) for x in (k.reshape(flat), v.reshape(flat), q.reshape(flat), proj.T)))
    count = tile * 2 * tile
    out = pl.pallas_call(
        functools.partial(decoder_kernel, rows, cols, tile),
        out_shape=jax.ShapeDtypeStruct((images, tile, 2, 2 * tile, chan), BF16),
        in_specs=[vmem] * 4 + [hbm],
        out_specs=pl.BlockSpec(memory_space=pl.ANY),
        scratch_shapes=[
            pltpu.VMEM(up.shape, BF16),
            pltpu.VMEM((wide * line, LANES), BF16),
            pltpu.VMEM(((wide - 2) * line, 3 * chan), BF16),
            pltpu.VMEM(((wide - 2) * line, chan), F32),
            pltpu.VMEM(((wide - 4) * line, chan), F32),
            pltpu.VMEM((3, (tile + 2) * 2 * tile, chan), BF16),
            pltpu.VMEM((5, chan, chan), BF16),
            pltpu.VMEM((chan // LANES, 2 * count, LANES), F32),
            pltpu.VMEM((2, images, tile, 2 * tile, chan), BF16),
            dma,
            dma((2,)),
        ],
        compiler_params=pltpu.CompilerParams(vmem_limit_bytes=36 * 1024 * 1024),
        name="decoder",
    )(ext, entry.reshape(3, -1, chan), gain.reshape(1, chan), res.reshape(3, -1, chan), pltpu.with_memory_space_constraint(up, pltpu.HBM))
    return out.reshape(images, 2 * tile, 2 * tile, chan)


def solution(mesh):
    spread = P(None, "row", "col", None)
    rows, cols = mesh.shape["row"], mesh.shape["col"]
    return jax.shard_map(
        functools.partial(local, rows, cols),
        mesh=mesh,
        in_specs=(spread,) * 3 + (P(),) * 5,
        out_specs=spread,
        check_vma=False,
    )
```
